256 devices in a mesh: ctx: 64 (over z, x, core), tp: 4 (over y).
Axes of the slice: x: 4, y: 4, z: 8, core: 2. Of those that a mesh axis runs over, the one named last changes fastest.
Arguments:
- context: bfloat16 [16384, 4096], P('ctx', 'tp'), may hold values from -6 to 6
- key_weight: bfloat16 [4096, 2048], P(None, 'tp'), may hold values from -0.09375 to 0.09375
- value_weight: bfloat16 [4096, 2048], P(None, 'tp'), may hold values from -0.09375 to 0.09375
- queries: bfloat16 [2048, 2048], P('ctx', 'tp'), may hold values from -64 to 64
- latent_pos: int32 [2048], replicated, may hold values from 0 to 16383, as said below
- out_grad: bfloat16 [2048, 2048], P('ctx', 'tp'), may hold values from -6 to 6
Outputs:
- attended: bfloat16 [2048, 2048], P('ctx', 'tp')
- context_grad: bfloat16 [16384, 4096], P('ctx', 'tp')
- query_grad: bfloat16 [2048, 2048], P('ctx', 'tp')
The draws below stay inside these ranges and needn't reach their ends.
Inputs may be any that keep to these rules, and one draw needn't show every extreme that they name: `latent_pos`: some latent sees the whole context and some latent sees only position 0.
All inputs are finite; a program needn't handle non-finite values.
Results may differ from the reference program's by a relative error of at most 0.025.
The reference program's roundings to bfloat16 on the way (of `key_rows`, `value_rows`, `weights`, `probs_low`, `value_grad`, `score_grad` and `key_grad`) count: a program that leaves them out, or rounds other values in their place, can miss the bound.
Values may be sent and summed in bfloat16 or wider, within the bound.
No kernel may reach another device: no remote copies, remote signals or barrier semaphores. Data moves between devices by JAX's collectives and lax.ppermute only.
A program may use at most 128 MiB of HBM per device.

```python
import math
import jax
import jax.numpy as jnp
from jax import lax

D = 4096
HEADS = 16
DH = 128
NCTX = 16384
LAT = 2048
HC = 2048


def draw_queries(key, part):
    key = jax.random.fold_in(key, 11)
    base_key = jax.random.fold_in(key, 0)
    base = jax.random.normal(base_key, (LAT, HEADS * DH), jnp.float32)
    return jnp.clip(base, -6.0, 6.0).astype(jnp.bfloat16)


def draw_latent_pos(key, part):
    key = jax.random.fold_in(key, 23)
    first_key, second_key = jax.random.split(key)
    chosen = jax.random.randint(first_key, (LAT,), 0, NCTX)
    places = jax.random.permutation(second_key, LAT)
    chosen = chosen.at[places[0]].set(NCTX - 1)
    chosen = chosen.at[places[1]].set(0)
    return chosen.astype(jnp.int32)


def level_of(own_key, shape, cuts, least, largest):
    gain, own = 1.0, jax.random.fold_in(own_key, 6)
    for dim, blocks in cuts:
        heights = jnp.exp(jax.random.uniform(jax.random.fold_in(own, dim), (blocks,), jnp.float32, least / len(cuts), largest / len(cuts)))
        gain = gain * jnp.repeat(heights, shape[dim] // blocks).reshape([-1 if axis == dim else 1 for axis in range(len(shape))])
    return gain


def noise(key, dims, spread, bound, cuts=(), kind=jnp.bfloat16):
    array = jax.random.normal(key, dims, jnp.float32) * spread
    if len(cuts) > 0:
        array = level_of(key, dims, cuts, -0.22, 0.18) * array
    return jnp.clip(array, min=-bound, max=bound).astype(kind)


def setup_inputs(seed: int = 0) -> dict:
    arg_keys = jax.random.split(jax.random.key(seed), 7)
    context = noise(arg_keys[0], (NCTX, D), 1.0, 6.0, ((0, 64), (1, 4)))
    key_weight = noise(arg_keys[1], (D, HC), D ** -0.5, 0.09375, ((1, 4),))
    value_weight = noise(arg_keys[2], (D, HC), D ** -0.5, 0.09375, ((1, 4),))
    queries = draw_queries(jax.random.fold_in(arg_keys[6], 71), 0)
    latent_pos = draw_latent_pos(jax.random.fold_in(arg_keys[6], 71), 0)
    out_grad = noise(arg_keys[5], (LAT, HC), 1.0, 6.0, ((0, 64), (1, 4)))
    return dict(context=context, key_weight=key_weight, value_weight=value_weight, queries=queries, latent_pos=latent_pos, out_grad=out_grad)


NEG_FILL = -1e+30

def reference(context, key_weight, value_weight, queries, latent_pos, out_grad):
    score_scale = 1.0 / math.sqrt(DH)
    key_rows = jnp.dot(context, key_weight, preferred_element_type=jnp.float32).astype(jnp.bfloat16)
    value_rows = jnp.dot(context, value_weight, preferred_element_type=jnp.float32).astype(jnp.bfloat16)
    positions = jnp.arange(NCTX, dtype=jnp.int32)
    allowed = positions[None, :] <= latent_pos[:, None].astype(jnp.int32)

    def by_head(matrix):
        return matrix.reshape(matrix.shape[0], HEADS, DH).transpose(1, 0, 2)

    def merged(stack):
        return stack.transpose(1, 0, 2).reshape(stack.shape[1], HEADS * DH)

    def one_head(operands):
        query_head, key_head, value_head, grad_head = operands
        scores = jnp.dot(query_head, key_head.T, preferred_element_type=jnp.float32) * score_scale
        row_peak = lax.optimization_barrier(jnp.max(jnp.where(allowed, scores, NEG_FILL), axis=1))
        expo = jnp.where(allowed, jnp.exp(scores - row_peak[:, None]), 0.0)
        denominator = lax.optimization_barrier(jnp.sum(expo, axis=1))
        weights = expo.astype(jnp.bfloat16)
        numer = jnp.dot(weights, value_head, preferred_element_type=jnp.float32)
        attended = (numer / denominator[:, None]).astype(jnp.bfloat16)
        log_norm = row_peak + jnp.log(denominator)
        grad_dot = lax.optimization_barrier(jnp.sum(grad_head.astype(jnp.float32) * attended.astype(jnp.float32), axis=1))
        probabilities = jnp.where(allowed, jnp.exp(scores - log_norm[:, None]), 0.0)
        probs_low = probabilities.astype(jnp.bfloat16)
        value_grad = jnp.dot(probs_low.T, grad_head, preferred_element_type=jnp.float32).astype(jnp.bfloat16)
        prob_grad = jnp.dot(grad_head, value_head.T, preferred_element_type=jnp.float32)
        score_grad = (probabilities * (prob_grad - grad_dot[:, None]) * score_scale).astype(jnp.bfloat16)
        key_grad = jnp.dot(score_grad.T, query_head, preferred_element_type=jnp.float32).astype(jnp.bfloat16)
        query_grad = jnp.dot(score_grad, key_head, preferred_element_type=jnp.float32).astype(jnp.bfloat16)
        return (attended, value_grad, key_grad, query_grad)
    attended, value_grad, key_grad, query_grad = lax.map(one_head, (by_head(queries), by_head(key_rows), by_head(value_rows), by_head(out_grad)))
    context_grad = (jnp.dot(merged(key_grad), key_weight.T, preferred_element_type=jnp.float32) + jnp.dot(merged(value_grad), value_weight.T, preferred_element_type=jnp.float32)).astype(jnp.bfloat16)
    return (merged(attended), context_grad, merged(query_grad))
```

```python
import functools
import math

import jax
import jax.numpy as jnp
from jax import lax
from jax.experimental import pallas as pl
from jax.experimental.pallas import tpu as pltpu
from jax.sharding import PartitionSpec as P

DH = 128
NZ, NX, NC, NY = 8, 4, 2, 4
NEG_FILL = -1e30
SCORE_SCALE = 1.0 / math.sqrt(DH)
LOG2_SCALE = SCORE_SCALE * math.log2(math.e)
VMEM_LIMIT = 56 * 1024 * 1024
F32 = jnp.float32
BF16 = jnp.bfloat16
NT = (((1,), (1,)), ((), ()))


def place(z, x, c):
    return (z * NX + x) * NC + c


CORE_SWAP = [
    (place(z, x, c), place(z, x, 1 - c)) for z in range(NZ) for x in range(NX) for c in range(NC)
]
X_GROUPS = [[place(z, x, c) for x in range(NX)] for z in range(NZ) for c in range(NC)]
Z_GROUPS = [[place(z, x, c) for z in range(NZ)] for x in range(NX) for c in range(NC)]
ZX_GROUPS = [[place(z, x, c) for z in range(NZ) for x in range(NX)] for c in range(NC)]


def swap_cores(array):
    return lax.ppermute(array, "ctx", CORE_SWAP)


def shift_y(array, step):
    return lax.ppermute(array, "tp", [(i, (i + step) % NY) for i in range(NY)])


def exchange(array, groups):
    return lax.all_to_all(array, "ctx", 0, 0, tiled=True, axis_index_groups=groups)


def compiler_params(**kw):
    return pltpu.CompilerParams(vmem_limit_bytes=VMEM_LIMIT, **kw)


def project_kernel(first, last, chunk_ref, x_ref, wk_ref, wv_ref, *refs):
    if first:
        out_ref, acc_ref = refs
    else:
        sum_ref, out_ref, acc_ref = refs
    step = pl.program_id(0)
    cols = wk_ref.shape[1]

    @pl.when(step == 0)
    def _():
        acc_ref[...] = jnp.zeros_like(acc_ref) if first else sum_ref[...]

    x = x_ref[...]
    acc_ref[:, :cols] += jnp.dot(x, wk_ref[...], preferred_element_type=F32)
    acc_ref[:, cols:] += jnp.dot(x, wv_ref[...], preferred_element_type=F32)

    @pl.when(step == pl.num_programs(0) - 1)
    def _():
        if last:
            for head in range(cols // DH):
                for kind in range(2):
                    at = kind * cols + head * DH
                    out_ref[head, kind] = acc_ref[:, at : at + DH].astype(BF16)
        else:
            out_ref[...] = acc_ref[...]


def project(chunk, x, wk, wv, total, last):
    rows, depth = x.shape
    cols = wk.shape[1]
    steps = 2
    tile = depth // steps
    first = total is None
    in_specs = [
        pl.BlockSpec((rows, tile), lambda i, ch: (0, i)),
        pl.BlockSpec((tile, cols), lambda i, ch: (ch[0] * steps + i, 0)),
        pl.BlockSpec((tile, cols), lambda i, ch: (ch[0] * steps + i, 0)),
    ]
    args = [x, wk, wv]
    if not first:
        in_specs.append(pl.BlockSpec((rows, 2 * cols), lambda i, ch: (0, 0)))
        args.append(total)
    if last:
        out_shape = jax.ShapeDtypeStruct((cols // DH, 2, rows, DH), BF16)
        out_spec = pl.BlockSpec((cols // DH, 2, rows, DH), lambda i, ch: (0, 0, 0, 0))
    else:
        out_shape = jax.ShapeDtypeStruct((rows, 2 * cols), F32)
        out_spec = pl.BlockSpec((rows, 2 * cols), lambda i, ch: (0, 0))
    return pl.pallas_call(
        functools.partial(project_kernel, first, last),
        out_shape=out_shape,
        grid_spec=pltpu.PrefetchScalarGridSpec(
            num_scalar_prefetch=1,
            grid=(steps,),
            in_specs=in_specs,
            out_specs=out_spec,
            scratch_shapes=[pltpu.VMEM((rows, 2 * cols), F32)],
        ),
        compiler_params=compiler_params(),
        cost_estimate=pl.CostEstimate(
            flops=4 * rows * depth * cols, bytes_accessed=4 * depth * cols, transcendentals=0
        ),
        name="project",
    )(chunk, *args)


BLOCK = 256


def masked_scores(base, kv_ref, q, lp):
    parts, rows = kv_ref.shape[0], kv_ref.shape[2]
    out = []
    for part in range(parts):
        scores = lax.dot_general(kv_ref[part, 0], q, NT, preferred_element_type=F32) * LOG2_SCALE
        rank = lax.broadcasted_iota(jnp.int32, (rows, BLOCK), 0)
        limit = lp - (base + part * NC * rows)
        out.append(jnp.where(rank <= limit, scores, NEG_FILL))
    return out


def row_pair(ref, *index):
    *lead, row = index
    return jnp.concatenate([ref[(*lead, pl.ds(row + k, 1))] for k in range(BLOCK // 128)], axis=1)


def stats_kernel(base_ref, kv_ref, own_ref, other_ref, lp_ref, out_ref):
    base = base_ref[0]
    parts = kv_ref.shape[0]
    per = own_ref.shape[0] // BLOCK
    lanes = BLOCK // 128
    for half, src in enumerate((own_ref, other_ref)):
        for block in range(per):
            at = pl.ds(block * BLOCK, BLOCK)
            q = src[at, :DH]
            go = src[at, DH:]
            lp = row_pair(lp_ref, half, block * lanes)
            scores = masked_scores(base, kv_ref, q, lp)
            peak = functools.reduce(
                jnp.maximum, [jnp.max(s, axis=0, keepdims=True) for s in scores]
            )
            total = 0.0
            dots = 0.0
            for part in range(parts):
                expo = jnp.exp2(scores[part] - peak)
                grads = lax.dot_general(kv_ref[part, 1], go, NT, preferred_element_type=F32)
                total += jnp.sum(expo, axis=0, keepdims=True)
                dots += jnp.sum(expo * grads, axis=0, keepdims=True)
            seen = peak > 0.5 * NEG_FILL
            total = jnp.where(seen, total, 0.0)
            dots = jnp.where(seen, dots, 0.0)
            for kind, value in enumerate((peak, total, dots)):
                for k in range(lanes):
                    out_ref[kind, half, pl.ds(block * lanes + k, 1)] = value[
                        :, k * 128 : (k + 1) * 128
                    ]


def latent_stats(base, kv, own, other, lp):
    groups = own.shape[0] // 128
    whole = pl.BlockSpec(memory_space=pltpu.VMEM)
    tokens = kv.shape[0] * kv.shape[2]
    work = tokens * 2 * own.shape[0]
    return pl.pallas_call(
        stats_kernel,
        out_shape=jax.ShapeDtypeStruct((3, 2, groups, 128), F32),
        in_specs=[pl.BlockSpec(memory_space=pltpu.SMEM)] + [whole] * 4,
        out_specs=whole,
        compiler_params=compiler_params(),
        cost_estimate=pl.CostEstimate(
            flops=4 * work * DH, bytes_accessed=2 * 2**20, transcendentals=work
        ),
        name="latent_stats",
    )(base, kv, own, other, lp)


def backward_kernel(
    base_ref, kv_ref, own_ref, other_ref, lp_ref, st_ref, dkv_ref, own_out, other_out,
    kvt_ref, acc_ref, fin_ref,
):
    base = base_ref[0]
    parts, rows = kv_ref.shape[0], kv_ref.shape[2]
    per = own_ref.shape[0] // BLOCK
    lanes = BLOCK // 128
    for part in range(parts):
        at = pl.ds(part * rows, rows)
        for kind in range(2):
            kvt_ref[kind, :, at] = kv_ref[part, kind].T
    acc_ref[...] = jnp.zeros_like(acc_ref)

    peaks = [st_ref[n, 0] for n in range(NZ)]
    top = functools.reduce(jnp.maximum, peaks)
    total = 0.0
    dots = 0.0
    for n in range(NZ):
        share = jnp.exp2(peaks[n] - top)
        total += share * st_ref[n, 1]
        dots += share * st_ref[n, 2]
    fin_ref[0] = top
    fin_ref[1] = jnp.log2(total)
    fin_ref[2] = dots / total

    for half, (src, dst) in enumerate(((own_ref, own_out), (other_ref, other_out))):
        for block in range(per):
            at = pl.ds(block * BLOCK, BLOCK)
            q = src[at, :DH]
            go = src[at, DH:]
            lp = row_pair(lp_ref, half, block * lanes)
            peak = row_pair(fin_ref, 0, half, block * lanes)
            log_total = row_pair(fin_ref, 1, half, block * lanes)
            dot = row_pair(fin_ref, 2, half, block * lanes)
            scores = masked_scores(base, kv_ref, q, lp)
            attended = 0.0
            query_grad = 0.0
            for part in range(parts):
                rows_at = pl.ds(part * rows, rows)
                probs = jnp.exp2((scores[part] - peak) - log_total)
                low = probs.astype(BF16)
                grads = lax.dot_general(kv_ref[part, 1], go, NT, preferred_element_type=F32)
                score_grad = (probs * (grads - dot) * SCORE_SCALE).astype(BF16)
                acc_ref[part, 1] += jnp.dot(low, go, preferred_element_type=F32)
                acc_ref[part, 0] += jnp.dot(score_grad, q, preferred_element_type=F32)
                attended += jnp.dot(kvt_ref[1, :, rows_at], low, preferred_element_type=F32)
                query_grad += jnp.dot(kvt_ref[0, :, rows_at], score_grad, preferred_element_type=F32)
            dst[at, :DH] = attended.T.astype(dst.dtype)
            dst[at, DH:] = query_grad.T.astype(dst.dtype)
    dkv_ref[...] = acc_ref[...].astype(BF16)


def backward(base, kv, own, other, lp, stats):
    whole = pl.BlockSpec(memory_space=pltpu.VMEM)
    parts, _, rows, _ = kv.shape
    work = parts * rows * 2 * own.shape[0]
    return pl.pallas_call(
        backward_kernel,
        out_shape=(
            jax.ShapeDtypeStruct(kv.shape, BF16),
            jax.ShapeDtypeStruct(own.shape, F32),
            jax.ShapeDtypeStruct(own.shape, BF16),
        ),
        in_specs=[pl.BlockSpec(memory_space=pltpu.SMEM)] + [whole] * 5,
        out_specs=(whole, whole, whole),
        scratch_shapes=[
            pltpu.VMEM((2, DH, parts * rows), BF16),
            pltpu.VMEM(kv.shape, F32),
            pltpu.VMEM(stats.shape[1:], F32),
        ],
        compiler_params=compiler_params(),
        cost_estimate=pl.CostEstimate(
            flops=12 * work * DH, bytes_accessed=5 * 2**20, transcendentals=work
        ),
        name="backward",
    )(base, kv, own, other, lp, stats)


def context_grad_kernel(chunk_ref, dkv_ref, wk_ref, wv_ref, out_ref):
    heads = dkv_ref.shape[0]
    dk = jnp.concatenate([dkv_ref[head, 0] for head in range(heads)], axis=1)
    dv = jnp.concatenate([dkv_ref[head, 1] for head in range(heads)], axis=1)
    total = lax.dot_general(dk, wk_ref[...], NT, preferred_element_type=F32)
    total += lax.dot_general(dv, wv_ref[...], NT, preferred_element_type=F32)
    out_ref[...] = total.astype(out_ref.dtype)


def context_term(chunk, dkv, wk, wv, dtype):
    heads, _, rows, _ = dkv.shape
    depth, cols = wk.shape
    width = depth // NY
    steps = 2
    tile = width // steps
    return pl.pallas_call(
        context_grad_kernel,
        out_shape=jax.ShapeDtypeStruct((rows, width), dtype),
        grid_spec=pltpu.PrefetchScalarGridSpec(
            num_scalar_prefetch=1,
            grid=(steps,),
            in_specs=[
                pl.BlockSpec(dkv.shape, lambda i, ch: (0, 0, 0, 0)),
                pl.BlockSpec((tile, cols), lambda i, ch: (ch[0] * steps + i, 0)),
                pl.BlockSpec((tile, cols), lambda i, ch: (ch[0] * steps + i, 0)),
            ],
            out_specs=pl.BlockSpec((rows, tile), lambda i, ch: (0, i)),
        ),
        compiler_params=compiler_params(),
        cost_estimate=pl.CostEstimate(
            flops=4 * rows * width * cols, bytes_accessed=4 * width * cols, transcendentals=0
        ),
        name="context_term",
    )(chunk, dkv, wk, wv)


def shards(context, key_weight, value_weight, queries, latent_pos, out_grad):
    rows = context.shape[0]
    lat = queries.shape[0]
    heads = key_weight.shape[1] // DH
    me = lax.axis_index("ctx")
    y = lax.axis_index("tp")
    z, core = me // (NX * NC), me % NC
    own_lat = NZ * NX * lat

    ahead = shift_y(context, 1)
    behind = shift_y(context, -1)
    across = shift_y(context, 2)

    def chunk(step):
        return lax.rem(y + step + NY, NY).astype(jnp.int32).reshape(1)

    both = jnp.concatenate(
        [queries.reshape(lat, heads, DH), out_grad.reshape(lat, heads, DH)], axis=2
    ).transpose(1, 0, 2)
    own = exchange(
        jnp.broadcast_to(both[None], (NZ, heads, lat, 2 * DH)).reshape(NZ * heads, lat, 2 * DH),
        ZX_GROUPS,
    ).reshape(own_lat, 2 * DH)
    other = swap_cores(own)

    by_core = latent_pos.reshape(NZ * NX, NC, lat).transpose(1, 0, 2).reshape(NC, own_lat)
    lp = jnp.where(core == 0, by_core, by_core[::-1]).reshape(NC, own_lat // 128, 128)
    base = ((z * NX * NC + core) * rows).astype(jnp.int32).reshape(1)

    total = project(chunk(0), context, key_weight, value_weight, None, False)
    total = project(chunk(-1), ahead, key_weight, value_weight, total, False)
    total = project(chunk(1), behind, key_weight, value_weight, total, False)
    kv = project(chunk(2), across, key_weight, value_weight, total, True)
    kv = exchange(kv, X_GROUPS)

    stats = latent_stats(base, kv, own, other, lp)
    theirs = swap_cores(stats)[:, ::-1]
    peak = jnp.maximum(stats[0], theirs[0])
    mine_share = jnp.exp2(stats[0] - peak)
    their_share = jnp.exp2(theirs[0] - peak)
    joined = jnp.stack([peak] + [stats[k] * mine_share + theirs[k] * their_share for k in (1, 2)])
    every = exchange(jnp.broadcast_to(joined[None], (NZ, *joined.shape)), Z_GROUPS)

    dkv, own_part, other_part = backward(base, kv, own, other, lp, every)
    received = swap_cores(other_part)
    dkv = exchange(dkv, X_GROUPS)

    send_across = context_term(chunk(2), dkv, key_weight, value_weight, BF16)
    got_across = shift_y(send_across, 2)
    send_ahead = context_term(chunk(1), dkv, key_weight, value_weight, BF16)
    got_ahead = shift_y(send_ahead, 1)
    send_behind = context_term(chunk(-1), dkv, key_weight, value_weight, BF16)
    got_behind = shift_y(send_behind, -1)
    kept = context_term(chunk(0), dkv, key_weight, value_weight, F32)

    parts = (own_part + received.astype(F32)).astype(BF16)
    parts = exchange(parts.reshape(NZ * NX, lat, 2 * DH), ZX_GROUPS)
    sums = jnp.sum(parts.reshape(NZ, heads, lat, 2 * DH).astype(F32), axis=0)
    sums = sums.astype(BF16).transpose(1, 0, 2)
    attended = sums[:, :, :DH].reshape(lat, heads * DH)
    query_grad = sums[:, :, DH:].reshape(lat, heads * DH)

    context_grad = (
        kept + got_across.astype(F32) + got_ahead.astype(F32) + got_behind.astype(F32)
    ).astype(BF16)
    return (attended, context_grad, query_grad)


def solution(mesh):
    return jax.shard_map(
        shards,
        mesh=mesh,
        in_specs=(
            P("ctx", "tp"),
            P(None, "tp"),
            P(None, "tp"),
            P("ctx", "tp"),
            P(),
            P("ctx", "tp"),
        ),
        out_specs=(P("ctx", "tp"), P("ctx", "tp"), P("ctx", "tp")),
        check_vma=False,
    )
```

```python
import functools
import math

import jax
import jax.numpy as jnp
from jax import lax
from jax.experimental import pallas as pl
from jax.experimental.pallas import tpu as pltpu
from jax.sharding import PartitionSpec as P

DH = 128
NZ, NX, NC, NY = 8, 4, 2, 4
NEG_FILL = -1e30
SCORE_SCALE = 1.0 / math.sqrt(DH)
LOG2_SCALE = SCORE_SCALE * math.log2(math.e)
VMEM_LIMIT = 16 * 1024 * 1024
F32 = jnp.float32
BF16 = jnp.bfloat16
NT = (((1,), (1,)), ((), ()))


def place(z, x, c):
    return (z * NX + x) * NC + c


CORE_SWAP = [
    (place(z, x, c), place(z, x, 1 - c)) for z in range(NZ) for x in range(NX) for c in range(NC)
]
Z_GROUPS = [[place(z, x, c) for z in range(NZ)] for x in range(NX) for c in range(NC)]


def swap_cores(array):
    return lax.ppermute(array, "ctx", CORE_SWAP)


def shift_y(array, step):
    return lax.ppermute(array, "tp", [(i, (i + step) % NY) for i in range(NY)])


def shift_x(array, step):
    pairs = [
        (place(z, x, c), place(z, (x + step) % NX, c))
        for z in range(NZ)
        for x in range(NX)
        for c in range(NC)
    ]
    return lax.ppermute(array, "ctx", pairs)


def flip_z(array, bit):
    pairs = [
        (place(z, x, c), place(z ^ bit, x, c))
        for z in range(NZ)
        for x in range(NX)
        for c in range(NC)
    ]
    return lax.ppermute(array, "ctx", pairs)


def exchange(array, groups):
    return lax.all_to_all(array, "ctx", 0, 0, tiled=True, axis_index_groups=groups)


FLIPS = (0, 4, 2, 6, 1, 5, 3, 7)


def compiler_params(limit=VMEM_LIMIT):
    return pltpu.CompilerParams(vmem_limit_bytes=limit)


def chunk_rows(at_ref, step, depth):
    return pl.ds(pl.multiple_of(lax.rem(at_ref[0] + step, NY) * depth, depth), depth)


def head_columns(at_ref, turn, heads):
    return pl.ds(pl.multiple_of(lax.rem(at_ref[1] + turn, heads) * DH, DH), DH)


def cost(flops, size, exponentials):
    return pl.CostEstimate(flops=0, bytes_accessed=0, transcendentals=0)


def load_weights_kernel(*refs):
    sources, targets, sem = refs[:2], refs[2:4], refs[4]
    copies = [pltpu.make_async_copy(*pair, sem.at[n]) for n, pair in enumerate(zip(sources, targets))]
    for copy in copies:
        copy.start()
    for copy in copies:
        copy.wait()


def load_weights(wk, wv):
    return pl.pallas_call(
        load_weights_kernel,
        out_shape=[jax.ShapeDtypeStruct(w.shape, w.dtype) for w in (wk, wv)],
        in_specs=[pl.BlockSpec(memory_space=pltpu.HBM)] * 2,
        out_specs=[pl.BlockSpec(memory_space=pltpu.VMEM)] * 2,
        scratch_shapes=[pltpu.SemaphoreType.DMA((2,))],
        compiler_params=compiler_params(),
        cost_estimate=cost(0, 4 * wk.size, 0),
        name="load_weights",
    )(wk, wv)


def project_kernel(steps, first, last, at_ref, *refs):
    wk_ref, wv_ref, refs = refs[0], refs[1], refs[2:]
    depth, cols = refs[0].shape[1], wk_ref.shape[1]
    total = [0.0, 0.0]
    refs = list(refs)
    pieces = []
    for step, count in steps:
        pieces.append(jnp.concatenate([refs.pop(0)[...] for _ in range(count)]))
    if not first:
        before = refs.pop(0)
        total = [before[kind] for kind in range(2)]
    for (step, _), piece in zip(steps, pieces):
        at = chunk_rows(at_ref, step, depth)
        for kind, weight in enumerate((wk_ref, wv_ref)):
            total[kind] += jnp.dot(piece, weight[at, :], preferred_element_type=F32)
    if last:
        heads = cols // DH
        outs, low_ref = refs[-heads - 1 : -1], refs[-1]
        for kind in range(2):
            low_ref[kind] = total[kind].astype(BF16)
        for turn, out in enumerate(outs):
            for kind in range(2):
                out[kind] = low_ref[kind, :, head_columns(at_ref, turn, heads)]
    else:
        for kind in range(2):
            refs[-1][kind] = total[kind]


def project(at, wk, wv, pieces, total, last):
    arrays = [array for group in pieces.values() for array in group]
    steps = tuple((step, len(group)) for step, group in pieces.items())
    depth = arrays[0].shape[1]
    rows = sum(array.shape[0] for array in arrays) // len(pieces)
    cols = wk.shape[1]
    first = total is None
    args = [wk, wv, *arrays] + ([] if first else [total])
    if last:
        out_shape = [jax.ShapeDtypeStruct((2, rows, DH), BF16)] * (cols // DH)
    else:
        out_shape = [jax.ShapeDtypeStruct((2, rows, cols), F32)]
    whole = pl.BlockSpec(memory_space=pltpu.VMEM)
    return pl.pallas_call(
        functools.partial(project_kernel, steps, first, last),
        out_shape=out_shape,
        in_specs=[pl.BlockSpec(memory_space=pltpu.SMEM)] + [whole] * len(args),
        out_specs=[whole] * len(out_shape),
        scratch_shapes=[pltpu.VMEM((2, rows, cols), BF16)] if last else [],
        compiler_params=compiler_params(),
        cost_estimate=cost(4 * len(pieces) * rows * depth * cols, 2**20, 0),
        name="project",
    )(at, *args)


BLOCK = 256
LANES = BLOCK // 128


def masked_scores(first, keys, q, lp):
    scores = lax.dot_general(keys, q, NT, preferred_element_type=F32) * LOG2_SCALE
    rank = lax.broadcasted_iota(jnp.int32, scores.shape, 0)
    return jnp.where(rank <= lp - first, scores, NEG_FILL)


def first_position(at_ref, turn, rows):
    return place(at_ref[2], lax.rem(at_ref[1] - turn + NX, NX), at_ref[3]) * rows


def row_of(at_ref, ref, *index):
    *lead, block = index
    parts = [
        ref[(*lead, pl.ds(at_ref[2] ^ FLIPS[block * LANES + k], 1))] for k in range(LANES)
    ]
    return jnp.concatenate(parts, axis=1)


def stats_kernel(at_ref, *refs):
    kv_refs, (own_ref, other_ref, lp_ref, out_ref) = refs[:NX], refs[NX:]
    rows = kv_refs[0].shape[1]
    for half, src in enumerate((own_ref, other_ref)):
        for block in range(src.shape[0] // BLOCK):
            at = pl.ds(block * BLOCK, BLOCK)
            q = src[at, :DH]
            go = src[at, DH:]
            lp = row_of(at_ref, lp_ref, half, block)
            scores = [masked_scores(first_position(at_ref, n, rows), kv_refs[n][0], q, lp) for n in range(NX)]
            peak = functools.reduce(
                jnp.maximum, [jnp.max(s, axis=0, keepdims=True) for s in scores]
            )
            total = 0.0
            dots = 0.0
            for n in range(NX):
                expo = jnp.exp2(scores[n] - peak)
                grads = lax.dot_general(kv_refs[n][1], go, NT, preferred_element_type=F32)
                total += jnp.sum(expo, axis=0, keepdims=True)
                dots += jnp.sum(expo * grads, axis=0, keepdims=True)
            seen = peak > 0.5 * NEG_FILL
            total = jnp.where(seen, total, 0.0)
            dots = jnp.where(seen, dots, 0.0)
            for kind, value in enumerate((peak, total, dots)):
                for k in range(LANES):
                    out_ref[kind, half, pl.ds(at_ref[2] ^ FLIPS[block * LANES + k], 1)] = value[
                        :, k * 128 : (k + 1) * 128
                    ]


def latent_stats(at, kv, own, other, lp):
    whole = pl.BlockSpec(memory_space=pltpu.VMEM)
    work = NX * kv[0].shape[1] * 2 * own.shape[0]
    return pl.pallas_call(
        stats_kernel,
        out_shape=jax.ShapeDtypeStruct((3, 2, own.shape[0] // 128, 128), F32),
        in_specs=[pl.BlockSpec(memory_space=pltpu.SMEM)] + [whole] * (NX + 3),
        out_specs=whole,
        compiler_params=compiler_params(),
        cost_estimate=cost(4 * work * DH, 2 * 2**20, work),
        name="latent_stats",
    )(at, *kv, own, other, lp)


def backward_kernel(at_ref, *refs):
    kv_refs, refs = refs[:NX], refs[NX:]
    rows = kv_refs[0].shape[1]
    (own_ref, other_ref, lp_ref, st_ref), refs = refs[:4], refs[4:]
    dkv_refs, (own_out, other_out, kvt_ref, acc_ref, fin_ref) = refs[:NX], refs[NX:]
    for n in range(NX):
        for kind in range(2):
            kvt_ref[n, kind] = kv_refs[n][kind].T
    acc_ref[...] = jnp.zeros_like(acc_ref)

    peaks = [st_ref[n, 0] for n in range(NZ)]
    top = functools.reduce(jnp.maximum, peaks)
    total = 0.0
    dots = 0.0
    for n in range(NZ):
        share = jnp.exp2(peaks[n] - top)
        total += share * st_ref[n, 1]
        dots += share * st_ref[n, 2]
    fin_ref[0] = top
    fin_ref[1] = jnp.log2(total)
    fin_ref[2] = dots / total

    for half, (src, dst) in enumerate(((own_ref, own_out), (other_ref, other_out))):
        for block in range(src.shape[0] // BLOCK):
            at = pl.ds(block * BLOCK, BLOCK)
            q = src[at, :DH]
            go = src[at, DH:]
            lp = row_of(at_ref, lp_ref, half, block)
            peak, log_total, dot = (row_of(at_ref, fin_ref, k, half, block) for k in range(3))
            attended = 0.0
            query_grad = 0.0
            for n in range(NX):
                scores = masked_scores(first_position(at_ref, n, rows), kv_refs[n][0], q, lp)
                probs = jnp.exp2((scores - peak) - log_total)
                low = probs.astype(BF16)
                grads = lax.dot_general(kv_refs[n][1], go, NT, preferred_element_type=F32)
                score_grad = (probs * (grads - dot) * SCORE_SCALE).astype(BF16)
                acc_ref[n, 1] += jnp.dot(low, go, preferred_element_type=F32)
                acc_ref[n, 0] += jnp.dot(score_grad, q, preferred_element_type=F32)
                attended += jnp.dot(kvt_ref[n, 1], low, preferred_element_type=F32)
                query_grad += jnp.dot(kvt_ref[n, 0], score_grad, preferred_element_type=F32)
            dst[at, :DH] = attended.T.astype(dst.dtype)
            dst[at, DH:] = query_grad.T.astype(dst.dtype)
    for n in range(NX):
        dkv_refs[n][...] = acc_ref[n].astype(BF16)


def backward(at, kv, own, other, lp, stats):
    whole = pl.BlockSpec(memory_space=pltpu.VMEM)
    rows = kv[0].shape[1]
    work = NX * rows * 2 * own.shape[0]
    out = pl.pallas_call(
        backward_kernel,
        out_shape=[jax.ShapeDtypeStruct(kv[0].shape, BF16)] * NX
        + [jax.ShapeDtypeStruct(own.shape, F32), jax.ShapeDtypeStruct(own.shape, BF16)],
        in_specs=[pl.BlockSpec(memory_space=pltpu.SMEM)] + [whole] * (NX + 4),
        out_specs=[whole] * (NX + 2),
        scratch_shapes=[
            pltpu.VMEM((NX, 2, DH, rows), BF16),
            pltpu.VMEM((NX, *kv[0].shape), F32),
            pltpu.VMEM(stats.shape[1:], F32),
        ],
        compiler_params=compiler_params(),
        cost_estimate=cost(12 * work * DH, 5 * 2**20, work),
        name="backward",
    )(at, *kv, own, other, lp, stats)
    return out[:NX], out[NX], out[NX + 1]


def context_grad_kernel(steps, halves, at_ref, wk_ref, wv_ref, *refs):
    dkv_refs, out_refs, grads_ref = refs[:NX], refs[NX:-1], refs[-1]
    for turn, ref in enumerate(dkv_refs):
        for kind in range(2):
            grads_ref[kind, :, head_columns(at_ref, turn, NX)] = ref[kind]
    for n, step in enumerate(steps):
        at = chunk_rows(at_ref, step, out_refs[0].shape[1])
        total = lax.dot_general(grads_ref[0], wk_ref[at, :], NT, preferred_element_type=F32)
        total += lax.dot_general(grads_ref[1], wv_ref[at, :], NT, preferred_element_type=F32)
        size = out_refs[0].shape[0]
        for k in range(halves):
            out = out_refs[n * halves + k]
            out[...] = total[k * size : (k + 1) * size].astype(out.dtype)


def context_terms(at, wk, wv, dkv, steps, halves, dtype):
    rows = dkv[0].shape[1]
    width, cols = wk.shape[0] // NY, wk.shape[1]
    whole = pl.BlockSpec(memory_space=pltpu.VMEM)
    count = len(steps) * halves
    return pl.pallas_call(
        functools.partial(context_grad_kernel, steps, halves),
        out_shape=[jax.ShapeDtypeStruct((rows // halves, width), dtype)] * count,
        in_specs=[pl.BlockSpec(memory_space=pltpu.SMEM)] + [whole] * (NX + 2),
        out_specs=[whole] * count,
        scratch_shapes=[pltpu.VMEM((2, rows, cols), BF16)],
        compiler_params=compiler_params(),
        cost_estimate=cost(4 * rows * width * cols * len(steps), 2**20, 0),
        name="context_terms",
    )(at, wk, wv, *dkv)


def join_kernel(up_ref, down_ref, upper_ref, lower_ref, up_out, down_out):
    half = upper_ref.shape[0]
    up_out[:half] = (up_ref[:half] + upper_ref[...].astype(F32)).astype(up_out.dtype)
    up_out[half:] = up_ref[half:].astype(up_out.dtype)
    down_out[:half] = down_ref[:half].astype(down_out.dtype)
    down_out[half:] = (down_ref[half:] + lower_ref[...].astype(F32)).astype(down_out.dtype)


def join_terms(up, down, upper, lower):
    whole = pl.BlockSpec(memory_space=pltpu.VMEM)
    return pl.pallas_call(
        join_kernel,
        out_shape=[jax.ShapeDtypeStruct(up.shape, BF16)] * 2,
        in_specs=[whole] * 4,
        out_specs=[whole] * 2,
        compiler_params=compiler_params(),
        cost_estimate=cost(0, 2**20, 0),
        name="join_terms",
    )(up, down, upper, lower)


def finish_kernel(kept_ref, up_ref, down_ref, out_ref):
    total = kept_ref[...] + up_ref[...].astype(F32) + down_ref[...].astype(F32)
    out_ref[...] = total.astype(out_ref.dtype)


def finish(kept, up, down):
    whole = pl.BlockSpec(memory_space=pltpu.VMEM)
    return pl.pallas_call(
        finish_kernel,
        out_shape=jax.ShapeDtypeStruct(kept.shape, BF16),
        in_specs=[whole] * 3,
        out_specs=whole,
        compiler_params=compiler_params(),
        cost_estimate=cost(0, 2**20, 0),
        name="finish",
    )(kept, up, down)


def shards(context, key_weight, value_weight, queries, latent_pos, out_grad):
    lat = queries.shape[0]
    heads = key_weight.shape[1] // DH
    me = lax.axis_index("ctx").astype(jnp.int32)
    y = lax.axis_index("tp").astype(jnp.int32)
    z, x, core = me >> 3, (me >> 1) & 3, me & 1
    at = jnp.stack([y, x, z, core])

    lp = latent_pos.reshape(NZ, NX, NC, lat)[:, ::-1]
    lp = lax.dynamic_slice_in_dim(jnp.concatenate([lp, lp], axis=1), NX - 1 - x, NX, 1)
    lp = lp.transpose(2, 0, 1, 3).reshape(NC, NZ, NX * lat)
    lp = jnp.where(core == 0, lp, lp[::-1])
    at, lp = lax.optimization_barrier((at, lp))

    rows = context.shape[0]
    ahead, behind = shift_y(context, 1), shift_y(context, -1)
    weights = load_weights(key_weight, value_weight)
    (total,) = project(at, *weights, {0: [context]}, None, False)

    both = jnp.concatenate(
        [queries.reshape(lat, heads, DH), out_grad.reshape(lat, heads, DH)], axis=2
    ).transpose(1, 0, 2)
    both = jnp.concatenate([both, both])
    by_turn = [lax.dynamic_slice_in_dim(both, x + turn, 1, 0)[0] for turn in range(NX)]
    own = jnp.concatenate([by_turn[0]] + [shift_x(by_turn[n], n) for n in range(1, NX)])
    own = jnp.concatenate([own, flip_z(own, 4)])
    own, total, ahead, behind = lax.optimization_barrier((own, total, ahead, behind))
    far_upper, far_lower = shift_y(ahead[: rows // 2], 1), shift_y(behind[rows // 2 :], -1)
    own = jnp.concatenate([own, flip_z(own, 2)])
    (total,) = project(at, *weights, {3: [ahead], 1: [behind]}, total, False)
    own, total, far_upper, far_lower = lax.optimization_barrier((own, total, far_upper, far_lower))
    own = jnp.concatenate([own, flip_z(own, 1)])
    kv = project(at, *weights, {2: [far_upper, far_lower]}, total, True)
    own, kv = lax.optimization_barrier((own, kv))
    kv = [kv[0]] + [shift_x(kv[n], n) for n in range(1, NX)]
    other = swap_cores(own)

    stats = latent_stats(at, kv, own, other, lp)
    theirs = swap_cores(stats)[:, ::-1]
    peak = jnp.maximum(stats[0], theirs[0])
    mine_share = jnp.exp2(stats[0] - peak)
    their_share = jnp.exp2(theirs[0] - peak)
    joined = jnp.stack([peak] + [stats[k] * mine_share + theirs[k] * their_share for k in (1, 2)])
    every = exchange(jnp.broadcast_to(joined[None], (NZ, *joined.shape)), Z_GROUPS)

    dkv, own_part, other_part = backward(at, kv, own, other, lp, every)
    received = swap_cores(other_part)
    dkv = [dkv[0]] + [shift_x(dkv[n], -n) for n in range(1, NX)]

    def terms(steps, halves, dtype):
        return context_terms(at, *weights, dkv, steps, halves, dtype)

    def halve(part, bit):
        half = part.shape[0] // 2
        return part[:half] + flip_z(part[half:].astype(BF16), bit).astype(F32)

    far_upper, far_lower = terms((2,), 2, BF16)
    add_upper, add_lower = shift_y(far_upper, 1), shift_y(far_lower, -1)
    part = own_part + received.astype(F32)
    part = halve(part, 1)
    part, far_upper = lax.optimization_barrier((part, far_upper))
    part = halve(part, 2)

    up, down, kept = terms((1, 3, 0), 1, F32)
    part, up, down, kept = lax.optimization_barrier((part, up, down, kept))
    part = halve(part, 4)
    up, down = join_terms(up, down, add_upper, add_lower)
    from_below, from_above = shift_y(up, 1), shift_y(down, -1)
    part, up = lax.optimization_barrier((part, up))

    part = part.astype(BF16).reshape(NX, lat, 2 * DH)
    part = jnp.stack([part[0]] + [shift_x(part[n], -n) for n in range(1, NX)])
    part = lax.dynamic_slice_in_dim(jnp.concatenate([part, part]), (heads - x) & 3, heads, 0)
    part, kept = lax.optimization_barrier((part.transpose(1, 0, 2), kept))
    attended = part[:, :, :DH].reshape(lat, heads * DH)
    query_grad = part[:, :, DH:].reshape(lat, heads * DH)

    return (attended, finish(kept, from_below, from_above), query_grad)


def solution(mesh):
    return jax.shard_map(
        shards,
        mesh=mesh,
        in_specs=(
            P("ctx", "tp"),
            P(None, "tp"),
            P(None, "tp"),
            P("ctx", "tp"),
            P(),
            P("ctx", "tp"),
        ),
        out_specs=(P("ctx", "tp"), P("ctx", "tp"), P("ctx", "tp")),
        check_vma=False,
    )
```

```python
import functools
import math

import jax
import jax.numpy as jnp
from jax import lax
from jax.experimental import pallas as pl
from jax.experimental.pallas import tpu as pltpu
from jax.sharding import PartitionSpec as P

DH = 128
NZ, NX, NC, NY = 8, 4, 2, 4
NEG_FILL = -1e30
SCORE_SCALE = 1.0 / math.sqrt(DH)
LOG2_SCALE = SCORE_SCALE * math.log2(math.e)
VMEM_LIMIT = 16 * 1024 * 1024
F32 = jnp.float32
BF16 = jnp.bfloat16
NT = (((1,), (1,)), ((), ()))


def place(z, x, c):
    return (z * NX + x) * NC + c


CORE_SWAP = [
    (place(z, x, c), place(z, x, 1 - c)) for z in range(NZ) for x in range(NX) for c in range(NC)
]
Z_GROUPS = [[place(z, x, c) for z in range(NZ)] for x in range(NX) for c in range(NC)]


def after(array, *others):
    return lax.optimization_barrier((array, *others))[0]


def swap_cores(array):
    return lax.ppermute(array, "ctx", CORE_SWAP)


def shift_y(array, step):
    return lax.ppermute(array, "tp", [(i, (i + step) % NY) for i in range(NY)])


def shift_x(array, step):
    pairs = [
        (place(z, x, c), place(z, (x + step) % NX, c))
        for z in range(NZ)
        for x in range(NX)
        for c in range(NC)
    ]
    return lax.ppermute(array, "ctx", pairs)


def flip_z(array, bit):
    pairs = [
        (place(z, x, c), place(z ^ bit, x, c))
        for z in range(NZ)
        for x in range(NX)
        for c in range(NC)
    ]
    return lax.ppermute(array, "ctx", pairs)


def exchange(array, groups):
    return lax.all_to_all(array, "ctx", 0, 0, tiled=True, axis_index_groups=groups)


FLIPS = (0, 4, 2, 6, 1, 5, 3, 7)


def compiler_params(limit=VMEM_LIMIT):
    return pltpu.CompilerParams(vmem_limit_bytes=limit)


def chunk_rows(at_ref, step, depth):
    return pl.ds(pl.multiple_of(lax.rem(at_ref[0] + step, NY) * depth, depth), depth)


def head_columns(at_ref, turn, heads):
    return pl.ds(pl.multiple_of(lax.rem(at_ref[1] + turn, heads) * DH, DH), DH)


def cost(flops, size, exponentials):
    return pl.CostEstimate(flops=0, bytes_accessed=0, transcendentals=0)


def load_weights_kernel(at_ref, *refs):
    sources, targets, sem = refs[:2], refs[2:4], refs[4]
    copies = [pltpu.make_async_copy(*pair, sem.at[n]) for n, pair in enumerate(zip(sources, targets))]
    for copy in copies:
        copy.start()
    for copy in copies:
        copy.wait()


def load_weights(at, wk, wv):
    return pl.pallas_call(
        load_weights_kernel,
        out_shape=[jax.ShapeDtypeStruct(w.shape, w.dtype) for w in (wk, wv)],
        in_specs=[pl.BlockSpec(memory_space=pltpu.SMEM)] + [pl.BlockSpec(memory_space=pltpu.HBM)] * 2,
        out_specs=[pl.BlockSpec(memory_space=pltpu.VMEM)] * 2,
        scratch_shapes=[pltpu.SemaphoreType.DMA((2,))],
        compiler_params=compiler_params(),
        cost_estimate=cost(0, 4 * wk.size, 0),
        name="load_weights",
    )(at, wk, wv)


def project_kernel(steps, first, last, at_ref, *refs):
    wk_ref, wv_ref, refs = refs[0], refs[1], refs[2:]
    depth, cols = refs[0].shape[1], wk_ref.shape[1]
    total = [0.0, 0.0]
    refs = list(refs)
    pieces = []
    for step, count in steps:
        pieces.append(jnp.concatenate([refs.pop(0)[...] for _ in range(count)]))
    if not first:
        before = refs.pop(0)
        total = [before[kind] for kind in range(2)]
    for (step, _), piece in zip(steps, pieces):
        at = chunk_rows(at_ref, step, depth)
        for kind, weight in enumerate((wk_ref, wv_ref)):
            total[kind] += jnp.dot(piece, weight[at, :], preferred_element_type=F32)
    if last:
        heads = cols // DH
        outs, low_ref = refs[-heads - 1 : -1], refs[-1]
        for kind in range(2):
            low_ref[kind] = total[kind].astype(BF16)
        for turn, out in enumerate(outs):
            for kind in range(2):
                out[kind] = low_ref[kind, :, head_columns(at_ref, turn, heads)]
    else:
        for kind in range(2):
            refs[-1][kind] = total[kind]


def project(at, wk, wv, pieces, total, last):
    arrays = [array for group in pieces.values() for array in group]
    steps = tuple((step, len(group)) for step, group in pieces.items())
    depth = arrays[0].shape[1]
    rows = sum(array.shape[0] for array in arrays) // len(pieces)
    cols = wk.shape[1]
    first = total is None
    args = [wk, wv, *arrays] + ([] if first else [total])
    if last:
        out_shape = [jax.ShapeDtypeStruct((2, rows, DH), BF16)] * (cols // DH)
    else:
        out_shape = [jax.ShapeDtypeStruct((2, rows, cols), F32)]
    whole = pl.BlockSpec(memory_space=pltpu.VMEM)
    return pl.pallas_call(
        functools.partial(project_kernel, steps, first, last),
        out_shape=out_shape,
        in_specs=[pl.BlockSpec(memory_space=pltpu.SMEM)] + [whole] * len(args),
        out_specs=[whole] * len(out_shape),
        scratch_shapes=[pltpu.VMEM((2, rows, cols), BF16)] if last else [],
        compiler_params=compiler_params(),
        cost_estimate=cost(4 * len(pieces) * rows * depth * cols, 2**20, 0),
        name="project",
    )(at, *args)


BLOCK = 256
LANES = BLOCK // 128


def masked_scores(first, keys, q, lp):
    scores = lax.dot_general(keys, q, NT, preferred_element_type=F32) * LOG2_SCALE
    rank = lax.broadcasted_iota(jnp.int32, scores.shape, 0)
    return jnp.where(rank <= lp - first, scores, NEG_FILL)


def first_position(at_ref, turn, rows):
    return place(at_ref[2], lax.rem(at_ref[1] - turn + NX, NX), at_ref[3]) * rows


def row_of(at_ref, ref, *index):
    *lead, block = index
    parts = [
        ref[(*lead, pl.ds(at_ref[2] ^ FLIPS[block * LANES + k], 1))] for k in range(LANES)
    ]
    return jnp.concatenate(parts, axis=1)


def stats_kernel(at_ref, *refs):
    kv_refs, (own_ref, other_ref, lp_ref, out_ref, expo_ref, grads_ref) = refs[:NX], refs[NX:]
    rows = kv_refs[0].shape[1]
    for half, src in enumerate((own_ref, other_ref)):
        for block in range(src.shape[0] // BLOCK):
            at = pl.ds(block * BLOCK, BLOCK)
            q = src[at, :DH]
            go = src[at, DH:]
            lp = row_of(at_ref, lp_ref, half, block)
            scores = [masked_scores(first_position(at_ref, n, rows), kv_refs[n][0], q, lp) for n in range(NX)]
            peak = functools.reduce(
                jnp.maximum, [jnp.max(s, axis=0, keepdims=True) for s in scores]
            )
            total = 0.0
            dots = 0.0
            for n in range(NX):
                expo = jnp.exp2(scores[n] - peak)
                grads = lax.dot_general(kv_refs[n][1], go, NT, preferred_element_type=F32)
                expo_ref[half, block, n] = expo
                grads_ref[half, block, n] = grads
                total += jnp.sum(expo, axis=0, keepdims=True)
                dots += jnp.sum(expo * grads, axis=0, keepdims=True)
            seen = peak > 0.5 * NEG_FILL
            total = jnp.where(seen, total, 0.0)
            dots = jnp.where(seen, dots, 0.0)
            for kind, value in enumerate((peak, total, dots)):
                for k in range(LANES):
                    out_ref[kind, half, pl.ds(at_ref[2] ^ FLIPS[block * LANES + k], 1)] = value[
                        :, k * 128 : (k + 1) * 128
                    ]


def latent_stats(at, kv, own, other, lp):
    whole = pl.BlockSpec(memory_space=pltpu.VMEM)
    work = NX * kv[0].shape[1] * 2 * own.shape[0]
    return pl.pallas_call(
        stats_kernel,
        out_shape=[jax.ShapeDtypeStruct((3, 2, own.shape[0] // 128, 128), F32)]
        + [jax.ShapeDtypeStruct((2, own.shape[0] // BLOCK, NX, kv[0].shape[1], BLOCK), F32)] * 2,
        in_specs=[pl.BlockSpec(memory_space=pltpu.SMEM)] + [whole] * (NX + 3),
        out_specs=[whole] * 3,
        compiler_params=compiler_params(),
        cost_estimate=cost(4 * work * DH, 2 * 2**20, work),
        name="latent_stats",
    )(at, *kv, own, other, lp)


def backward_kernel(at_ref, *refs):
    kv_refs, refs = refs[:NX], refs[NX:]
    rows = kv_refs[0].shape[1]
    (own_ref, other_ref, expo_ref, grads_ref, mine_ref, st_ref), refs = refs[:6], refs[6:]
    dkv_refs, (own_out, other_out, kvt_ref, acc_ref, fin_ref) = refs[:NX], refs[NX:]
    for n in range(NX):
        for kind in range(2):
            kvt_ref[n, kind] = kv_refs[n][kind].T
    acc_ref[...] = jnp.zeros_like(acc_ref)

    peaks = [st_ref[n, 0] for n in range(NZ)]
    top = functools.reduce(jnp.maximum, peaks)
    total = 0.0
    dots = 0.0
    for n in range(NZ):
        share = jnp.exp2(peaks[n] - top)
        total += share * st_ref[n, 1]
        dots += share * st_ref[n, 2]
    fin_ref[0] = jnp.where(mine_ref[1] > 0.0, jnp.exp2(mine_ref[0] - top), 0.0) / total
    fin_ref[1] = dots / total

    for half, (src, dst) in enumerate(((own_ref, own_out), (other_ref, other_out))):
        for block in range(src.shape[0] // BLOCK):
            at = pl.ds(block * BLOCK, BLOCK)
            q = src[at, :DH]
            go = src[at, DH:]
            share, dot = (row_of(at_ref, fin_ref, k, half, block) for k in range(2))
            attended = 0.0
            query_grad = 0.0
            for n in range(NX):
                probs = expo_ref[half, block, n] * share
                low = probs.astype(BF16)
                grads = grads_ref[half, block, n]
                score_grad = (probs * (grads - dot) * SCORE_SCALE).astype(BF16)
                acc_ref[n, 1] += jnp.dot(low, go, preferred_element_type=F32)
                acc_ref[n, 0] += jnp.dot(score_grad, q, preferred_element_type=F32)
                attended += jnp.dot(kvt_ref[n, 1], low, preferred_element_type=F32)
                query_grad += jnp.dot(kvt_ref[n, 0], score_grad, preferred_element_type=F32)
            dst[at, :DH] = attended.T.astype(dst.dtype)
            dst[at, DH:] = query_grad.T.astype(dst.dtype)
    for n in range(NX):
        dkv_refs[n][...] = acc_ref[n].astype(BF16)


def backward(at, kv, own, other, expo, grads, mine, stats):
    whole = pl.BlockSpec(memory_space=pltpu.VMEM)
    rows = kv[0].shape[1]
    work = NX * rows * 2 * own.shape[0]
    out = pl.pallas_call(
        backward_kernel,
        out_shape=[jax.ShapeDtypeStruct(kv[0].shape, BF16)] * NX
        + [jax.ShapeDtypeStruct(own.shape, F32), jax.ShapeDtypeStruct(own.shape, BF16)],
        in_specs=[pl.BlockSpec(memory_space=pltpu.SMEM)] + [whole] * (NX + 6),
        out_specs=[whole] * (NX + 2),
        scratch_shapes=[
            pltpu.VMEM((NX, 2, DH, rows), BF16),
            pltpu.VMEM((NX, *kv[0].shape), F32),
            pltpu.VMEM((2, *stats.shape[2:]), F32),
        ],
        compiler_params=compiler_params(),
        cost_estimate=cost(8 * work * DH, 5 * 2**20, 0),
        name="backward",
    )(at, *kv, own, other, expo, grads, mine, stats)
    return out[:NX], out[NX], out[NX + 1]


def context_grad_kernel(steps, halves, at_ref, wk_ref, wv_ref, *refs):
    dkv_refs, out_refs, grads_ref = refs[:NX], refs[NX:-1], refs[-1]
    for turn, ref in enumerate(dkv_refs):
        for kind in range(2):
            grads_ref[kind, :, head_columns(at_ref, turn, NX)] = ref[kind]
    for n, step in enumerate(steps):
        at = chunk_rows(at_ref, step, out_refs[0].shape[1])
        total = lax.dot_general(grads_ref[0], wk_ref[at, :], NT, preferred_element_type=F32)
        total += lax.dot_general(grads_ref[1], wv_ref[at, :], NT, preferred_element_type=F32)
        size = out_refs[0].shape[0]
        for k in range(halves):
            out = out_refs[n * halves + k]
            out[...] = total[k * size : (k + 1) * size].astype(out.dtype)


def context_terms(at, wk, wv, dkv, steps, halves, dtype):
    rows = dkv[0].shape[1]
    width, cols = wk.shape[0] // NY, wk.shape[1]
    whole = pl.BlockSpec(memory_space=pltpu.VMEM)
    count = len(steps) * halves
    return pl.pallas_call(
        functools.partial(context_grad_kernel, steps, halves),
        out_shape=[jax.ShapeDtypeStruct((rows // halves, width), dtype)] * count,
        in_specs=[pl.BlockSpec(memory_space=pltpu.SMEM)] + [whole] * (NX + 2),
        out_specs=[whole] * count,
        scratch_shapes=[pltpu.VMEM((2, rows, cols), BF16)],
        compiler_params=compiler_params(),
        cost_estimate=cost(4 * rows * width * cols * len(steps), 2**20, 0),
        name="context_terms",
    )(at, wk, wv, *dkv)


def join_kernel(up_ref, down_ref, upper_ref, lower_ref, up_out, down_out):
    half = upper_ref.shape[0]
    up_out[:half] = (up_ref[:half] + upper_ref[...].astype(F32)).astype(up_out.dtype)
    up_out[half:] = up_ref[half:].astype(up_out.dtype)
    down_out[:half] = down_ref[:half].astype(down_out.dtype)
    down_out[half:] = (down_ref[half:] + lower_ref[...].astype(F32)).astype(down_out.dtype)


def join_terms(up, down, upper, lower):
    whole = pl.BlockSpec(memory_space=pltpu.VMEM)
    return pl.pallas_call(
        join_kernel,
        out_shape=[jax.ShapeDtypeStruct(up.shape, BF16)] * 2,
        in_specs=[whole] * 4,
        out_specs=[whole] * 2,
        compiler_params=compiler_params(),
        cost_estimate=cost(0, 2**20, 0),
        name="join_terms",
    )(up, down, upper, lower)


def finish_kernel(kept_ref, up_ref, down_ref, out_ref):
    total = kept_ref[...] + up_ref[...].astype(F32) + down_ref[...].astype(F32)
    out_ref[...] = total.astype(out_ref.dtype)


def finish(kept, up, down):
    whole = pl.BlockSpec(memory_space=pltpu.VMEM)
    return pl.pallas_call(
        finish_kernel,
        out_shape=jax.ShapeDtypeStruct(kept.shape, BF16),
        in_specs=[whole] * 3,
        out_specs=whole,
        compiler_params=compiler_params(),
        cost_estimate=cost(0, 2**20, 0),
        name="finish",
    )(kept, up, down)


def shards(context, key_weight, value_weight, queries, latent_pos, out_grad):
    lat = queries.shape[0]
    heads = key_weight.shape[1] // DH
    me = lax.axis_index("ctx").astype(jnp.int32)
    y = lax.axis_index("tp").astype(jnp.int32)
    z, x, core = me >> 3, (me >> 1) & 3, me & 1
    at = jnp.stack([y, x, z, core])

    lp = latent_pos.reshape(NZ, NX, NC, lat)[:, ::-1]
    lp = lax.dynamic_slice_in_dim(jnp.concatenate([lp, lp], axis=1), NX - 1 - x, NX, 1)
    lp = lp.transpose(2, 0, 1, 3).reshape(NC, NZ, NX * lat)
    lp = jnp.where(core == 0, lp, lp[::-1])
    at, lp = lax.optimization_barrier((at, lp))

    rows = context.shape[0]
    ahead, behind = shift_y(context, 1), shift_y(context, -1)

    both = jnp.concatenate(
        [queries.reshape(lat, heads, DH), out_grad.reshape(lat, heads, DH)], axis=2
    ).transpose(1, 0, 2)
    both = jnp.concatenate([both, both])
    by_turn = [lax.dynamic_slice_in_dim(both, x + turn, 1, 0)[0] for turn in range(NX)]
    own = jnp.concatenate([by_turn[0]] + [shift_x(by_turn[n], n) for n in range(1, NX)])
    got = [flip_z(own, bit) for bit in (4, 2, 6)]
    own = jnp.concatenate([own, *got])
    weights = load_weights(after(at, *got), key_weight, value_weight)
    (total,) = project(at, *weights, {0: [context]}, None, False)
    far_upper, far_lower = shift_y(ahead[: rows // 2], 1), shift_y(behind[rows // 2 :], -1)
    (total,) = project(at, *weights, {3: [ahead], 1: [behind]}, total, False)
    own = after(own, far_upper, far_lower, total)
    own = jnp.concatenate([own, flip_z(own, 1)])
    kv = project(at, *weights, {2: [far_upper, far_lower]}, total, True)
    kv = [kv[0]] + [shift_x(kv[n], n) for n in range(1, NX)]
    other = swap_cores(after(own, *kv[1:]))

    stats, expo, prob_grads = latent_stats(at, kv, own, other, lp)
    theirs = swap_cores(stats)[:, ::-1]
    peak = jnp.maximum(stats[0], theirs[0])
    mine_share = jnp.exp2(stats[0] - peak)
    their_share = jnp.exp2(theirs[0] - peak)
    joined = jnp.stack([peak] + [stats[k] * mine_share + theirs[k] * their_share for k in (1, 2)])
    every = exchange(jnp.broadcast_to(joined[None], (NZ, *joined.shape)), Z_GROUPS)

    dkv, own_part, other_part = backward(at, kv, own, other, expo, prob_grads, stats, every)
    received = swap_cores(other_part)
    dkv = [dkv[0]] + [shift_x(dkv[n], -n) for n in range(1, NX)]

    def terms(steps, halves, dtype):
        return context_terms(at, *weights, dkv, steps, halves, dtype)

    def halve(part, bit):
        half = part.shape[0] // 2
        return part[:half] + flip_z(part[half:].astype(BF16), bit).astype(F32)

    far_upper, far_lower = terms((2,), 2, BF16)
    add_upper, add_lower = shift_y(far_upper, 1), shift_y(far_lower, -1)
    part = own_part + received.astype(F32)
    part = halve(part, 1)
    part = halve(after(part, far_upper), 2)

    up, down, kept = terms((1, 3, 0), 1, F32)
    part = halve(after(part, kept), 4)
    up, down = join_terms(up, down, add_upper, add_lower)
    from_below, from_above = shift_y(up, 1), shift_y(down, -1)
    part = after(part, up)
    part = part.astype(BF16).reshape(NX, lat, 2 * DH)
    part = jnp.stack([part[0]] + [shift_x(part[n], -n) for n in range(1, NX)])
    part = lax.dynamic_slice_in_dim(jnp.concatenate([part, part]), (heads - x) & 3, heads, 0)
    part = part.transpose(1, 0, 2)
    kept = after(kept, part)
    attended = part[:, :, :DH].reshape(lat, heads * DH)
    query_grad = part[:, :, DH:].reshape(lat, heads * DH)

    return (attended, finish(kept, from_below, from_above), query_grad)


def solution(mesh):
    return jax.shard_map(
        shards,
        mesh=mesh,
        in_specs=(
            P("ctx", "tp"),
            P(None, "tp"),
            P(None, "tp"),
            P("ctx", "tp"),
            P(),
            P("ctx", "tp"),
        ),
        out_specs=(P("ctx", "tp"), P("ctx", "tp"), P("ctx", "tp")),
        check_vma=False,
    )
```

```python
import functools
import math

import jax
import jax.numpy as jnp
from jax import lax
from jax.experimental import pallas as pl
from jax.experimental.pallas import tpu as pltpu
from jax.sharding import PartitionSpec as P

DH = 128
NZ, NX, NC, NY = 8, 4, 2, 4
NEG_FILL = -1e30
SCORE_SCALE = 1.0 / math.sqrt(DH)
LOG2_SCALE = SCORE_SCALE * math.log2(math.e)
VMEM_LIMIT = 8 * 1024 * 1024
F32 = jnp.float32
BF16 = jnp.bfloat16
NT = (((1,), (1,)), ((), ()))


def place(z, x, c):
    return (z * NX + x) * NC + c


CORE_SWAP = [
    (place(z, x, c), place(z, x, 1 - c)) for z in range(NZ) for x in range(NX) for c in range(NC)
]
Z_GROUPS = [[place(z, x, c) for z in range(NZ)] for x in range(NX) for c in range(NC)]


def after(array, *others):
    return lax.optimization_barrier((array, *others))[0]


def swap_cores(array):
    return lax.ppermute(array, "ctx", CORE_SWAP)


def shift_y(array, step):
    return lax.ppermute(array, "tp", [(i, (i + step) % NY) for i in range(NY)])


def shift_x(array, step):
    pairs = [
        (place(z, x, c), place(z, (x + step) % NX, c))
        for z in range(NZ)
        for x in range(NX)
        for c in range(NC)
    ]
    return lax.ppermute(array, "ctx", pairs)


def flip_z(array, bit):
    pairs = [
        (place(z, x, c), place(z ^ bit, x, c))
        for z in range(NZ)
        for x in range(NX)
        for c in range(NC)
    ]
    return lax.ppermute(array, "ctx", pairs)


def exchange(array, groups):
    return lax.all_to_all(array, "ctx", 0, 0, tiled=True, axis_index_groups=groups)


FLIPS = (0, 4, 2, 6, 1, 5, 3, 7)


def compiler_params(limit=VMEM_LIMIT):
    return pltpu.CompilerParams(vmem_limit_bytes=limit)


def chunk_rows(at_ref, step, depth):
    return pl.ds(pl.multiple_of(lax.rem(at_ref[0] + step, NY) * depth, depth), depth)


def head_columns(at_ref, turn, heads):
    return pl.ds(pl.multiple_of(lax.rem(at_ref[1] + turn, heads) * DH, DH), DH)


def cost(flops, size, exponentials):
    return pl.CostEstimate(flops=0, bytes_accessed=0, transcendentals=0)


def load_weights_kernel(at_ref, *refs):
    sources, targets, sem = refs[:2], refs[2:4], refs[4]
    copies = [pltpu.make_async_copy(*pair, sem.at[n]) for n, pair in enumerate(zip(sources, targets))]
    for copy in copies:
        copy.start()
    for copy in copies:
        copy.wait()


def load_weights(at, wk, wv):
    return pl.pallas_call(
        load_weights_kernel,
        out_shape=[jax.ShapeDtypeStruct(w.shape, w.dtype) for w in (wk, wv)],
        in_specs=[pl.BlockSpec(memory_space=pltpu.SMEM)] + [pl.BlockSpec(memory_space=pltpu.HBM)] * 2,
        out_specs=[pl.BlockSpec(memory_space=pltpu.VMEM)] * 2,
        scratch_shapes=[pltpu.SemaphoreType.DMA((2,))],
        compiler_params=compiler_params(),
        cost_estimate=cost(0, 4 * wk.size, 0),
        name="load_weights",
    )(at, wk, wv)


def project_kernel(steps, first, last, at_ref, *refs):
    wk_ref, wv_ref, refs = refs[0], refs[1], refs[2:]
    depth, cols = refs[0].shape[1], wk_ref.shape[1]
    total = [0.0, 0.0]
    refs = list(refs)
    pieces = []
    for step, count in steps:
        pieces.append(jnp.concatenate([refs.pop(0)[...] for _ in range(count)]))
    if not first:
        before = refs.pop(0)
        total = [before[kind] for kind in range(2)]
    for (step, _), piece in zip(steps, pieces):
        at = chunk_rows(at_ref, step, depth)
        for kind, weight in enumerate((wk_ref, wv_ref)):
            total[kind] += jnp.dot(piece, weight[at, :], preferred_element_type=F32)
    if last:
        heads = cols // DH
        outs, low_ref = refs[-heads - 1 : -1], refs[-1]
        for kind in range(2):
            low_ref[kind] = total[kind].astype(BF16)
        for turn, out in enumerate(outs):
            for kind in range(2):
                out[kind] = low_ref[kind, :, head_columns(at_ref, turn, heads)]
    else:
        for kind in range(2):
            refs[-1][kind] = total[kind]


def project(at, wk, wv, pieces, total, last):
    arrays = [array for group in pieces.values() for array in group]
    steps = tuple((step, len(group)) for step, group in pieces.items())
    depth = arrays[0].shape[1]
    rows = sum(array.shape[0] for array in arrays) // len(pieces)
    cols = wk.shape[1]
    first = total is None
    args = [wk, wv, *arrays] + ([] if first else [total])
    if last:
        out_shape = [jax.ShapeDtypeStruct((2, rows, DH), BF16)] * (cols // DH)
    else:
        out_shape = [jax.ShapeDtypeStruct((2, rows, cols), F32)]
    whole = pl.BlockSpec(memory_space=pltpu.VMEM)
    return pl.pallas_call(
        functools.partial(project_kernel, steps, first, last),
        out_shape=out_shape,
        in_specs=[pl.BlockSpec(memory_space=pltpu.SMEM)] + [whole] * len(args),
        out_specs=[whole] * len(out_shape),
        scratch_shapes=[pltpu.VMEM((2, rows, cols), BF16)] if last else [],
        compiler_params=compiler_params(),
        cost_estimate=cost(4 * len(pieces) * rows * depth * cols, 2**20, 0),
        name="project",
    )(at, *args)


BLOCK = 256
LANES = BLOCK // 128


def masked_scores(first, keys, q, lp):
    scores = lax.dot_general(keys, q, NT, preferred_element_type=F32) * LOG2_SCALE
    rank = lax.broadcasted_iota(jnp.int32, scores.shape, 0)
    return jnp.where(rank <= lp - first, scores, NEG_FILL)


def first_position(at_ref, turn, rows):
    return place(at_ref[2], lax.rem(at_ref[1] - turn + NX, NX), at_ref[3]) * rows


def row_of(at_ref, ref, *index):
    *lead, block = index
    parts = [
        ref[(*lead, pl.ds(at_ref[2] ^ FLIPS[block * LANES + k], 1))] for k in range(LANES)
    ]
    return jnp.concatenate(parts, axis=1)


def stats_kernel(at_ref, *refs):
    kv_refs, (own_ref, other_ref, lp_ref, out_ref, expo_ref, grads_ref) = refs[:NX], refs[NX:]
    rows = kv_refs[0].shape[1]
    for half, src in enumerate((own_ref, other_ref)):
        for block in range(src.shape[0] // BLOCK):
            at = pl.ds(block * BLOCK, BLOCK)
            q = src[at, :DH]
            go = src[at, DH:]
            lp = row_of(at_ref, lp_ref, half, block)
            scores = [masked_scores(first_position(at_ref, n, rows), kv_refs[n][0], q, lp) for n in range(NX)]
            peak = functools.reduce(
                jnp.maximum, [jnp.max(s, axis=0, keepdims=True) for s in scores]
            )
            total = 0.0
            dots = 0.0
            for n in range(NX):
                expo = jnp.exp2(scores[n] - peak)
                grads = lax.dot_general(kv_refs[n][1], go, NT, preferred_element_type=F32)
                expo_ref[half, block, n] = expo
                grads_ref[half, block, n] = grads
                total += jnp.sum(expo, axis=0, keepdims=True)
                dots += jnp.sum(expo * grads, axis=0, keepdims=True)
            seen = peak > 0.5 * NEG_FILL
            total = jnp.where(seen, total, 0.0)
            dots = jnp.where(seen, dots, 0.0)
            for kind, value in enumerate((peak, total, dots)):
                for k in range(LANES):
                    out_ref[kind, half, pl.ds(at_ref[2] ^ FLIPS[block * LANES + k], 1)] = value[
                        :, k * 128 : (k + 1) * 128
                    ]


def latent_stats(at, kv, own, other, lp):
    whole = pl.BlockSpec(memory_space=pltpu.VMEM)
    work = NX * kv[0].shape[1] * 2 * own.shape[0]
    return pl.pallas_call(
        stats_kernel,
        out_shape=[jax.ShapeDtypeStruct((3, 2, own.shape[0] // 128, 128), F32)]
        + [jax.ShapeDtypeStruct((2, own.shape[0] // BLOCK, NX, kv[0].shape[1], BLOCK), F32)] * 2,
        in_specs=[pl.BlockSpec(memory_space=pltpu.SMEM)] + [whole] * (NX + 3),
        out_specs=[whole] * 3,
        compiler_params=compiler_params(),
        cost_estimate=cost(4 * work * DH, 2 * 2**20, work),
        name="latent_stats",
    )(at, *kv, own, other, lp)


def backward_kernel(at_ref, *refs):
    kv_refs, refs = refs[:NX], refs[NX:]
    rows = kv_refs[0].shape[1]
    (own_ref, other_ref, expo_ref, grads_ref, mine_ref, st_ref), refs = refs[:6], refs[6:]
    dkv_refs, (own_out, other_out, kvt_ref, acc_ref, fin_ref) = refs[:NX], refs[NX:]
    for n in range(NX):
        for kind in range(2):
            kvt_ref[n, kind] = kv_refs[n][kind].T
    acc_ref[...] = jnp.zeros_like(acc_ref)

    peaks = [st_ref[n, 0] for n in range(NZ)]
    top = functools.reduce(jnp.maximum, peaks)
    total = 0.0
    dots = 0.0
    for n in range(NZ):
        share = jnp.exp2(peaks[n] - top)
        total += share * st_ref[n, 1]
        dots += share * st_ref[n, 2]
    fin_ref[0] = jnp.where(mine_ref[1] > 0.0, jnp.exp2(mine_ref[0] - top), 0.0) / total
    fin_ref[1] = dots / total

    for half, (src, dst) in enumerate(((own_ref, own_out), (other_ref, other_out))):
        for block in range(src.shape[0] // BLOCK):
            at = pl.ds(block * BLOCK, BLOCK)
            q = src[at, :DH]
            go = src[at, DH:]
            share, dot = (row_of(at_ref, fin_ref, k, half, block) for k in range(2))
            attended = 0.0
            query_grad = 0.0
            for n in range(NX):
                probs = expo_ref[half, block, n] * share
                low = probs.astype(BF16)
                grads = grads_ref[half, block, n]
                score_grad = (probs * (grads - dot) * SCORE_SCALE).astype(BF16)
                acc_ref[n, 1] += jnp.dot(low, go, preferred_element_type=F32)
                acc_ref[n, 0] += jnp.dot(score_grad, q, preferred_element_type=F32)
                attended += jnp.dot(kvt_ref[n, 1], low, preferred_element_type=F32)
                query_grad += jnp.dot(kvt_ref[n, 0], score_grad, preferred_element_type=F32)
            dst[at, :DH] = attended.T.astype(dst.dtype)
            dst[at, DH:] = query_grad.T.astype(dst.dtype)
    for n in range(NX):
        dkv_refs[n][...] = acc_ref[n].astype(BF16)


def backward(at, kv, own, other, expo, grads, mine, stats):
    whole = pl.BlockSpec(memory_space=pltpu.VMEM)
    rows = kv[0].shape[1]
    work = NX * rows * 2 * own.shape[0]
    out = pl.pallas_call(
        backward_kernel,
        out_shape=[jax.ShapeDtypeStruct(kv[0].shape, BF16)] * NX
        + [jax.ShapeDtypeStruct(own.shape, F32), jax.ShapeDtypeStruct(own.shape, BF16)],
        in_specs=[pl.BlockSpec(memory_space=pltpu.SMEM)] + [whole] * (NX + 6),
        out_specs=[whole] * (NX + 2),
        scratch_shapes=[
            pltpu.VMEM((NX, 2, DH, rows), BF16),
            pltpu.VMEM((NX, *kv[0].shape), F32),
            pltpu.VMEM((2, *stats.shape[2:]), F32),
        ],
        compiler_params=compiler_params(),
        cost_estimate=cost(8 * work * DH, 5 * 2**20, 0),
        name="backward",
    )(at, *kv, own, other, expo, grads, mine, stats)
    return out[:NX], out[NX], out[NX + 1]


def context_grad_kernel(steps, halves, at_ref, wk_ref, wv_ref, *refs):
    dkv_refs, out_refs, grads_ref = refs[:NX], refs[NX:-1], refs[-1]
    for turn, ref in enumerate(dkv_refs):
        for kind in range(2):
            grads_ref[kind, :, head_columns(at_ref, turn, NX)] = ref[kind]
    for n, step in enumerate(steps):
        at = chunk_rows(at_ref, step, out_refs[0].shape[1])
        total = lax.dot_general(grads_ref[0], wk_ref[at, :], NT, preferred_element_type=F32)
        total += lax.dot_general(grads_ref[1], wv_ref[at, :], NT, preferred_element_type=F32)
        size = out_refs[0].shape[0]
        for k in range(halves):
            out = out_refs[n * halves + k]
            out[...] = total[k * size : (k + 1) * size].astype(out.dtype)


def context_terms(at, wk, wv, dkv, steps, halves, dtype):
    rows = dkv[0].shape[1]
    width, cols = wk.shape[0] // NY, wk.shape[1]
    whole = pl.BlockSpec(memory_space=pltpu.VMEM)
    count = len(steps) * halves
    return pl.pallas_call(
        functools.partial(context_grad_kernel, steps, halves),
        out_shape=[jax.ShapeDtypeStruct((rows // halves, width), dtype)] * count,
        in_specs=[pl.BlockSpec(memory_space=pltpu.SMEM)] + [whole] * (NX + 2),
        out_specs=[whole] * count,
        scratch_shapes=[pltpu.VMEM((2, rows, cols), BF16)],
        compiler_params=compiler_params(),
        cost_estimate=cost(4 * rows * width * cols * len(steps), 2**20, 0),
        name="context_terms",
    )(at, wk, wv, *dkv)


def join_kernel(up_ref, down_ref, upper_ref, lower_ref, up_out, down_out):
    half = upper_ref.shape[0]
    up_out[:half] = (up_ref[:half] + upper_ref[...].astype(F32)).astype(up_out.dtype)
    up_out[half:] = up_ref[half:].astype(up_out.dtype)
    down_out[:half] = down_ref[:half].astype(down_out.dtype)
    down_out[half:] = (down_ref[half:] + lower_ref[...].astype(F32)).astype(down_out.dtype)


def join_terms(up, down, upper, lower):
    whole = pl.BlockSpec(memory_space=pltpu.VMEM)
    return pl.pallas_call(
        join_kernel,
        out_shape=[jax.ShapeDtypeStruct(up.shape, BF16)] * 2,
        in_specs=[whole] * 4,
        out_specs=[whole] * 2,
        compiler_params=compiler_params(),
        cost_estimate=cost(0, 2**20, 0),
        name="join_terms",
    )(up, down, upper, lower)


def finish_kernel(kept_ref, up_ref, down_ref, out_ref):
    total = kept_ref[...] + up_ref[...].astype(F32) + down_ref[...].astype(F32)
    out_ref[...] = total.astype(out_ref.dtype)


def finish(kept, up, down):
    whole = pl.BlockSpec(memory_space=pltpu.VMEM)
    return pl.pallas_call(
        finish_kernel,
        out_shape=jax.ShapeDtypeStruct(kept.shape, BF16),
        in_specs=[whole] * 3,
        out_specs=whole,
        compiler_params=compiler_params(),
        cost_estimate=cost(0, 2**20, 0),
        name="finish",
    )(kept, up, down)


def place_heads_kernel(at_ref, *refs):
    pieces, outs = refs[:NX], refs[NX:]
    for turn, piece in enumerate(pieces):
        for kind, out in enumerate(outs):
            out[:, head_columns(at_ref, turn, NX)] = piece[:, kind * DH : (kind + 1) * DH]


def place_heads(at, pieces):
    whole = pl.BlockSpec(memory_space=pltpu.VMEM)
    shape = jax.ShapeDtypeStruct((pieces[0].shape[0], NX * DH), BF16)
    return pl.pallas_call(
        place_heads_kernel,
        out_shape=[shape, shape],
        in_specs=[pl.BlockSpec(memory_space=pltpu.SMEM)] + [whole] * NX,
        out_specs=[whole] * 2,
        compiler_params=compiler_params(),
        cost_estimate=cost(0, 2**17, 0),
        name="place_heads",
    )(at, *pieces)


def shards(context, key_weight, value_weight, queries, latent_pos, out_grad):
    lat = queries.shape[0]
    heads = key_weight.shape[1] // DH
    me = lax.axis_index("ctx").astype(jnp.int32)
    y = lax.axis_index("tp").astype(jnp.int32)
    z, x, core = me >> 3, (me >> 1) & 3, me & 1
    at = jnp.stack([y, x, z, core])

    lp = latent_pos.reshape(NZ, NX, NC, lat)[:, ::-1]
    lp = lax.dynamic_slice_in_dim(jnp.concatenate([lp, lp], axis=1), NX - 1 - x, NX, 1)
    lp = lp.transpose(2, 0, 1, 3).reshape(NC, NZ, NX * lat)
    lp = jnp.where(core == 0, lp, lp[::-1])
    at, lp = lax.optimization_barrier((at, lp))

    rows = context.shape[0]
    ahead, behind = shift_y(context, 1), shift_y(context, -1)

    both = jnp.concatenate(
        [queries.reshape(lat, heads, DH), out_grad.reshape(lat, heads, DH)], axis=2
    ).transpose(1, 0, 2)
    both = jnp.concatenate([both, both])
    by_turn = [lax.dynamic_slice_in_dim(both, x + turn, 1, 0)[0] for turn in range(NX)]
    own = jnp.concatenate([by_turn[0]] + [shift_x(by_turn[n], n) for n in range(1, NX)])
    got = [flip_z(own, bit) for bit in (4, 2, 6)]
    own = jnp.concatenate([own, *got])
    weights = load_weights(after(at, *got), key_weight, value_weight)
    (total,) = project(at, *weights, {0: [context]}, None, False)
    far_upper, far_lower = shift_y(ahead[: rows // 2], 1), shift_y(behind[rows // 2 :], -1)
    (total,) = project(at, *weights, {3: [ahead], 1: [behind]}, total, False)
    own = after(own, far_upper, far_lower, total)
    own = jnp.concatenate([own, flip_z(own, 1)])
    kv = project(at, *weights, {2: [far_upper, far_lower]}, total, True)
    kv = [kv[0]] + [shift_x(kv[n], n) for n in range(1, NX)]
    other = swap_cores(after(own, *kv[1:]))

    stats, expo, prob_grads = latent_stats(at, kv, own, other, lp)
    theirs = swap_cores(stats)[:, ::-1]
    peak = jnp.maximum(stats[0], theirs[0])
    mine_share = jnp.exp2(stats[0] - peak)
    their_share = jnp.exp2(theirs[0] - peak)
    joined = jnp.stack([peak] + [stats[k] * mine_share + theirs[k] * their_share for k in (1, 2)])
    every = exchange(jnp.broadcast_to(joined[None], (NZ, *joined.shape)), Z_GROUPS)

    dkv, own_part, other_part = backward(at, kv, own, other, expo, prob_grads, stats, every)
    received = swap_cores(other_part)
    dkv = [dkv[0]] + [shift_x(dkv[n], -n) for n in range(1, NX)]

    def terms(steps, halves, dtype):
        return context_terms(at, *weights, dkv, steps, halves, dtype)

    def halve(part, bit):
        half = part.shape[0] // 2
        return part[:half] + flip_z(part[half:].astype(BF16), bit).astype(F32)

    far_upper, far_lower = terms((2,), 2, BF16)
    add_upper, add_lower = shift_y(far_upper, 1), shift_y(far_lower, -1)
    part = own_part + received.astype(F32)
    part = halve(part, 1)
    part = halve(after(part, far_upper), 2)

    up, down, kept = terms((1, 3, 0), 1, F32)
    part = halve(after(part, kept), 4)
    up, down = join_terms(up, down, add_upper, add_lower)
    from_below, from_above = shift_y(up, 1), shift_y(down, -1)
    part = after(part, up)
    part = part.astype(BF16).reshape(NX, lat, 2 * DH)
    pieces = [part[0]] + [shift_x(part[n], -n) for n in range(1, NX)]
    attended, query_grad = place_heads(at, pieces)
    kept = after(kept, attended)

    return (attended, finish(kept, from_below, from_above), query_grad)


def solution(mesh):
    return jax.shard_map(
        shards,
        mesh=mesh,
        in_specs=(
            P("ctx", "tp"),
            P(None, "tp"),
            P(None, "tp"),
            P("ctx", "tp"),
            P(),
            P("ctx", "tp"),
        ),
        out_specs=(P("ctx", "tp"), P("ctx", "tp"), P("ctx", "tp")),
        check_vma=False,
    )
```

```python
import functools
import math

import jax
import jax.numpy as jnp
from jax import lax
from jax.experimental import pallas as pl
from jax.experimental.pallas import tpu as pltpu
from jax.sharding import PartitionSpec as P

DH = 128
NZ, NX, NC, NY = 8, 4, 2, 4
NEG_FILL = -1e30
SCORE_SCALE = 1.0 / math.sqrt(DH)
LOG2_SCALE = SCORE_SCALE * math.log2(math.e)
VMEM_LIMIT = 8 * 1024 * 1024
F32 = jnp.float32
BF16 = jnp.bfloat16
NT = (((1,), (1,)), ((), ()))


def place(z, x, c):
    return (z * NX + x) * NC + c


CORE_SWAP = [
    (place(z, x, c), place(z, x, 1 - c)) for z in range(NZ) for x in range(NX) for c in range(NC)
]
Z_GROUPS = [[place(z, x, c) for z in range(NZ)] for x in range(NX) for c in range(NC)]


def after(array, *others):
    return lax.optimization_barrier((array, *others))[0]


def swap_cores(array):
    return lax.ppermute(array, "ctx", CORE_SWAP)


def shift_y(array, step):
    return lax.ppermute(array, "tp", [(i, (i + step) % NY) for i in range(NY)])


def shift_x(array, step):
    pairs = [
        (place(z, x, c), place(z, (x + step) % NX, c))
        for z in range(NZ)
        for x in range(NX)
        for c in range(NC)
    ]
    return lax.ppermute(array, "ctx", pairs)


def flip_z(array, bit):
    pairs = [
        (place(z, x, c), place(z ^ bit, x, c))
        for z in range(NZ)
        for x in range(NX)
        for c in range(NC)
    ]
    return lax.ppermute(array, "ctx", pairs)


def exchange(array, groups):
    return lax.all_to_all(array, "ctx", 0, 0, tiled=True, axis_index_groups=groups)


FLIPS = (0, 4, 2, 6, 1, 5, 3, 7)


def compiler_params(limit=VMEM_LIMIT):
    return pltpu.CompilerParams(vmem_limit_bytes=limit)


def chunk_rows(at_ref, step, depth):
    return pl.ds(pl.multiple_of(lax.rem(at_ref[0] + step, NY) * depth, depth), depth)


def head_columns(at_ref, turn, heads):
    return pl.ds(pl.multiple_of(lax.rem(at_ref[1] + turn, heads) * DH, DH), DH)


def cost(flops, size, exponentials):
    return pl.CostEstimate(flops=0, bytes_accessed=0, transcendentals=0)


def load_weights_kernel(at_ref, *refs):
    sources, targets, sem = refs[:2], refs[2:4], refs[4]
    copies = [pltpu.make_async_copy(*pair, sem.at[n]) for n, pair in enumerate(zip(sources, targets))]
    for copy in copies:
        copy.start()
    for copy in copies:
        copy.wait()


def load_weights(at, wk, wv):
    return pl.pallas_call(
        load_weights_kernel,
        out_shape=[jax.ShapeDtypeStruct(w.shape, w.dtype) for w in (wk, wv)],
        in_specs=[pl.BlockSpec(memory_space=pltpu.SMEM)] + [pl.BlockSpec(memory_space=pltpu.HBM)] * 2,
        out_specs=[pl.BlockSpec(memory_space=pltpu.VMEM)] * 2,
        scratch_shapes=[pltpu.SemaphoreType.DMA((2,))],
        compiler_params=compiler_params(),
        cost_estimate=cost(0, 4 * wk.size, 0),
        name="load_weights",
    )(at, wk, wv)


def project_kernel(steps, first, last, at_ref, *refs):
    wk_ref, wv_ref, refs = refs[0], refs[1], refs[2:]
    depth, cols = refs[0].shape[1], wk_ref.shape[1]
    total = [0.0, 0.0]
    refs = list(refs)
    pieces = []
    for step, count in steps:
        pieces.append(jnp.concatenate([refs.pop(0)[...] for _ in range(count)]))
    if not first:
        before = refs.pop(0)
        total = [before[kind] for kind in range(2)]
    for (step, _), piece in zip(steps, pieces):
        at = chunk_rows(at_ref, step, depth)
        for kind, weight in enumerate((wk_ref, wv_ref)):
            total[kind] += jnp.dot(piece, weight[at, :], preferred_element_type=F32)
    if last:
        heads = cols // DH
        outs, low_ref = refs[-heads - 1 : -1], refs[-1]
        for kind in range(2):
            low_ref[kind] = total[kind].astype(BF16)
        for turn, out in enumerate(outs):
            for kind in range(2):
                out[kind] = low_ref[kind, :, head_columns(at_ref, turn, heads)]
    else:
        for kind in range(2):
            refs[-1][kind] = total[kind]


def project(at, wk, wv, pieces, total, last):
    arrays = [array for group in pieces.values() for array in group]
    steps = tuple((step, len(group)) for step, group in pieces.items())
    depth = arrays[0].shape[1]
    rows = sum(array.shape[0] for array in arrays) // len(pieces)
    cols = wk.shape[1]
    first = total is None
    args = [wk, wv, *arrays] + ([] if first else [total])
    if last:
        out_shape = [jax.ShapeDtypeStruct((2, rows, DH), BF16)] * (cols // DH)
    else:
        out_shape = [jax.ShapeDtypeStruct((2, rows, cols), F32)]
    whole = pl.BlockSpec(memory_space=pltpu.VMEM)
    return pl.pallas_call(
        functools.partial(project_kernel, steps, first, last),
        out_shape=out_shape,
        in_specs=[pl.BlockSpec(memory_space=pltpu.SMEM)] + [whole] * len(args),
        out_specs=[whole] * len(out_shape),
        scratch_shapes=[pltpu.VMEM((2, rows, cols), BF16)] if last else [],
        compiler_params=compiler_params(),
        cost_estimate=cost(4 * len(pieces) * rows * depth * cols, 2**20, 0),
        name="project",
    )(at, *args)


BLOCK = 256
LANES = BLOCK // 128


def masked_scores(first, keys, q, lp):
    scores = lax.dot_general(keys, q, NT, preferred_element_type=F32) * LOG2_SCALE
    rank = lax.broadcasted_iota(jnp.int32, scores.shape, 0)
    return jnp.where(rank <= lp - first, scores, NEG_FILL)


def first_position(at_ref, turn, rows):
    return place(at_ref[2], lax.rem(at_ref[1] - turn + NX, NX), at_ref[3]) * rows


def row_of(at_ref, ref, *index):
    *lead, block = index
    parts = [
        ref[(*lead, pl.ds(at_ref[2] ^ FLIPS[block * LANES + k], 1))] for k in range(LANES)
    ]
    return jnp.concatenate(parts, axis=1)


def stats_kernel(at_ref, *refs):
    kv_refs, (own_ref, other_ref, lp_ref, out_ref, expo_ref, grads_ref) = refs[:NX], refs[NX:]
    rows = kv_refs[0].shape[1]
    for half, src in enumerate((own_ref, other_ref)):
        for block in range(src.shape[0] // BLOCK):
            at = pl.ds(block * BLOCK, BLOCK)
            q = src[at, :DH]
            go = src[at, DH:]
            lp = row_of(at_ref, lp_ref, half, block)
            scores = [masked_scores(first_position(at_ref, n, rows), kv_refs[n][0], q, lp) for n in range(NX)]
            peak = functools.reduce(
                jnp.maximum, [jnp.max(s, axis=0, keepdims=True) for s in scores]
            )
            total = 0.0
            dots = 0.0
            for n in range(NX):
                expo = jnp.exp2(scores[n] - peak)
                grads = lax.dot_general(kv_refs[n][1], go, NT, preferred_element_type=F32)
                expo_ref[half, block, n] = expo
                grads_ref[half, block, n] = grads
                total += jnp.sum(expo, axis=0, keepdims=True)
                dots += jnp.sum(expo * grads, axis=0, keepdims=True)
            seen = peak > 0.5 * NEG_FILL
            total = jnp.where(seen, total, 0.0)
            dots = jnp.where(seen, dots, 0.0)
            for kind, value in enumerate((peak, total, dots)):
                for k in range(LANES):
                    out_ref[kind, half, pl.ds(at_ref[2] ^ FLIPS[block * LANES + k], 1)] = value[
                        :, k * 128 : (k + 1) * 128
                    ]


def latent_stats(at, kv, own, other, lp):
    whole = pl.BlockSpec(memory_space=pltpu.VMEM)
    work = NX * kv[0].shape[1] * 2 * own.shape[0]
    return pl.pallas_call(
        stats_kernel,
        out_shape=[jax.ShapeDtypeStruct((3, 2, own.shape[0] // 128, 128), F32)]
        + [jax.ShapeDtypeStruct((2, own.shape[0] // BLOCK, NX, kv[0].shape[1], BLOCK), F32)] * 2,
        in_specs=[pl.BlockSpec(memory_space=pltpu.SMEM)] + [whole] * (NX + 3),
        out_specs=[whole] * 3,
        compiler_params=compiler_params(),
        cost_estimate=cost(4 * work * DH, 2 * 2**20, work),
        name="latent_stats",
    )(at, *kv, own, other, lp)


def backward_kernel(at_ref, *refs):
    kv_refs, refs = refs[:NX], refs[NX:]
    rows = kv_refs[0].shape[1]
    (own_ref, other_ref, expo_ref, grads_ref, mine_ref, st_ref), refs = refs[:6], refs[6:]
    dkv_refs, (own_out, other_out, kvt_ref, acc_ref, fin_ref) = refs[:NX], refs[NX:]
    for n in range(NX):
        for kind in range(2):
            kvt_ref[n, kind] = kv_refs[n][kind].T
    acc_ref[...] = jnp.zeros_like(acc_ref)

    peaks = [st_ref[n, 0] for n in range(NZ)]
    top = functools.reduce(jnp.maximum, peaks)
    total = 0.0
    dots = 0.0
    for n in range(NZ):
        share = jnp.exp2(peaks[n] - top)
        total += share * st_ref[n, 1]
        dots += share * st_ref[n, 2]
    fin_ref[0] = jnp.where(mine_ref[1] > 0.0, jnp.exp2(mine_ref[0] - top), 0.0) / total
    fin_ref[1] = dots / total

    for half, (src, dst) in enumerate(((own_ref, own_out), (other_ref, other_out))):
        for block in range(src.shape[0] // BLOCK):
            at = pl.ds(block * BLOCK, BLOCK)
            q = src[at, :DH]
            go = src[at, DH:]
            share, dot = (row_of(at_ref, fin_ref, k, half, block) for k in range(2))
            attended = 0.0
            query_grad = 0.0
            for n in range(NX):
                probs = expo_ref[half, block, n] * share
                low = probs.astype(BF16)
                grads = grads_ref[half, block, n]
                score_grad = (probs * (grads - dot) * SCORE_SCALE).astype(BF16)
                acc_ref[n, 1] += jnp.dot(low, go, preferred_element_type=F32)
                acc_ref[n, 0] += jnp.dot(score_grad, q, preferred_element_type=F32)
                attended += jnp.dot(kvt_ref[n, 1], low, preferred_element_type=F32)
                query_grad += jnp.dot(kvt_ref[n, 0], score_grad, preferred_element_type=F32)
            dst[at, :DH] = attended.T.astype(dst.dtype)
            dst[at, DH:] = query_grad.T.astype(dst.dtype)
    for n in range(NX):
        dkv_refs[n][...] = acc_ref[n].astype(BF16)


def backward(at, kv, own, other, expo, grads, mine, stats):
    whole = pl.BlockSpec(memory_space=pltpu.VMEM)
    rows = kv[0].shape[1]
    work = NX * rows * 2 * own.shape[0]
    out = pl.pallas_call(
        backward_kernel,
        out_shape=[jax.ShapeDtypeStruct(kv[0].shape, BF16)] * NX
        + [jax.ShapeDtypeStruct(own.shape, F32), jax.ShapeDtypeStruct(own.shape, BF16)],
        in_specs=[pl.BlockSpec(memory_space=pltpu.SMEM)] + [whole] * (NX + 6),
        out_specs=[whole] * (NX + 2),
        scratch_shapes=[
            pltpu.VMEM((NX, 2, DH, rows), BF16),
            pltpu.VMEM((NX, *kv[0].shape), F32),
            pltpu.VMEM((2, *stats.shape[2:]), F32),
        ],
        compiler_params=compiler_params(),
        cost_estimate=cost(8 * work * DH, 5 * 2**20, 0),
        name="backward",
    )(at, *kv, own, other, expo, grads, mine, stats)
    return out[:NX], out[NX], out[NX + 1]


def context_grad_kernel(steps, halves, at_ref, wk_ref, wv_ref, *refs):
    dkv_refs, out_refs, grads_ref = refs[:NX], refs[NX:-1], refs[-1]
    for turn, ref in enumerate(dkv_refs):
        for kind in range(2):
            grads_ref[kind, :, head_columns(at_ref, turn, NX)] = ref[kind]
    for n, step in enumerate(steps):
        at = chunk_rows(at_ref, step, out_refs[0].shape[1])
        total = lax.dot_general(grads_ref[0], wk_ref[at, :], NT, preferred_element_type=F32)
        total += lax.dot_general(grads_ref[1], wv_ref[at, :], NT, preferred_element_type=F32)
        size = out_refs[0].shape[0]
        for k in range(halves):
            out = out_refs[n * halves + k]
            out[...] = total[k * size : (k + 1) * size].astype(out.dtype)


def context_terms(at, wk, wv, dkv, steps, halves, dtype):
    rows = dkv[0].shape[1]
    width, cols = wk.shape[0] // NY, wk.shape[1]
    whole = pl.BlockSpec(memory_space=pltpu.VMEM)
    count = len(steps) * halves
    return pl.pallas_call(
        functools.partial(context_grad_kernel, steps, halves),
        out_shape=[jax.ShapeDtypeStruct((rows // halves, width), dtype)] * count,
        in_specs=[pl.BlockSpec(memory_space=pltpu.SMEM)] + [whole] * (NX + 2),
        out_specs=[whole] * count,
        scratch_shapes=[pltpu.VMEM((2, rows, cols), BF16)],
        compiler_params=compiler_params(),
        cost_estimate=cost(4 * rows * width * cols * len(steps), 2**20, 0),
        name="context_terms",
    )(at, wk, wv, *dkv)


def join_kernel(up_ref, down_ref, upper_ref, lower_ref, up_out, down_out):
    half = upper_ref.shape[0]
    up_out[:half] = (up_ref[:half] + upper_ref[...].astype(F32)).astype(up_out.dtype)
    up_out[half:] = up_ref[half:].astype(up_out.dtype)
    down_out[:half] = down_ref[:half].astype(down_out.dtype)
    down_out[half:] = (down_ref[half:] + lower_ref[...].astype(F32)).astype(down_out.dtype)


def join_terms(up, down, upper, lower):
    whole = pl.BlockSpec(memory_space=pltpu.VMEM)
    return pl.pallas_call(
        join_kernel,
        out_shape=[jax.ShapeDtypeStruct(up.shape, BF16)] * 2,
        in_specs=[whole] * 4,
        out_specs=[whole] * 2,
        compiler_params=compiler_params(),
        cost_estimate=cost(0, 2**20, 0),
        name="join_terms",
    )(up, down, upper, lower)


def finish_kernel(kept_ref, up_ref, down_ref, out_ref):
    total = kept_ref[...] + up_ref[...].astype(F32) + down_ref[...].astype(F32)
    out_ref[...] = total.astype(out_ref.dtype)


def finish(kept, up, down):
    whole = pl.BlockSpec(memory_space=pltpu.VMEM)
    return pl.pallas_call(
        finish_kernel,
        out_shape=jax.ShapeDtypeStruct(kept.shape, BF16),
        in_specs=[whole] * 3,
        out_specs=whole,
        compiler_params=compiler_params(),
        cost_estimate=cost(0, 2**20, 0),
        name="finish",
    )(kept, up, down)


def place_heads_kernel(at_ref, *refs):
    pieces, outs = refs[:NX], refs[NX:]
    for turn, piece in enumerate(pieces):
        for kind, out in enumerate(outs):
            out[:, head_columns(at_ref, turn, NX)] = piece[:, kind * DH : (kind + 1) * DH]


def place_heads(at, pieces):
    whole = pl.BlockSpec(memory_space=pltpu.VMEM)
    shape = jax.ShapeDtypeStruct((pieces[0].shape[0], NX * DH), BF16)
    return pl.pallas_call(
        place_heads_kernel,
        out_shape=[shape, shape],
        in_specs=[pl.BlockSpec(memory_space=pltpu.SMEM)] + [whole] * NX,
        out_specs=[whole] * 2,
        compiler_params=compiler_params(),
        cost_estimate=cost(0, 2**17, 0),
        name="place_heads",
    )(at, *pieces)


def shards(context, key_weight, value_weight, queries, latent_pos, out_grad):
    lat = queries.shape[0]
    heads = key_weight.shape[1] // DH
    me = lax.axis_index("ctx").astype(jnp.int32)
    y = lax.axis_index("tp").astype(jnp.int32)
    z, x, core = me >> 3, (me >> 1) & 3, me & 1
    at = jnp.stack([y, x, z, core])

    lp = latent_pos.reshape(NZ, NX, NC, lat)[:, ::-1]
    lp = lax.dynamic_slice_in_dim(jnp.concatenate([lp, lp], axis=1), NX - 1 - x, NX, 1)
    lp = lp.transpose(2, 0, 1, 3).reshape(NC, NZ, NX * lat)
    lp = jnp.where(core == 0, lp, lp[::-1])
    at, lp = lax.optimization_barrier((at, lp))

    rows = context.shape[0]
    ahead, behind = shift_y(context, 1), shift_y(context, -1)

    both = jnp.concatenate(
        [queries.reshape(lat, heads, DH), out_grad.reshape(lat, heads, DH)], axis=2
    ).transpose(1, 0, 2)
    both = jnp.concatenate([both, both])
    by_turn = [lax.dynamic_slice_in_dim(both, x + turn, 1, 0)[0] for turn in range(NX)]
    own = jnp.concatenate([by_turn[0]] + [shift_x(by_turn[n], n) for n in range(1, NX)])
    got = [flip_z(own, bit) for bit in (4, 2, 6)]
    own = jnp.concatenate([own, *got])
    weights = load_weights(after(at, *got), key_weight, value_weight)
    far_upper, far_lower = shift_y(ahead[: rows // 2], 1), shift_y(behind[rows // 2 :], -1)
    pieces = {0: [context], 3: [ahead], 1: [behind]}
    (total,) = project(at, *weights, pieces, None, False)
    own = after(own, far_upper, far_lower, total)
    own = jnp.concatenate([own, flip_z(own, 1)])
    kv = project(at, *weights, {2: [far_upper, far_lower]}, total, True)
    kv = [kv[0]] + [shift_x(kv[n], n) for n in range(1, NX)]
    other = swap_cores(after(own, *kv[1:]))

    stats, expo, prob_grads = latent_stats(at, kv, own, other, lp)
    theirs = swap_cores(stats)[:, ::-1]
    peak = jnp.maximum(stats[0], theirs[0])
    mine_share = jnp.exp2(stats[0] - peak)
    their_share = jnp.exp2(theirs[0] - peak)
    joined = jnp.stack([peak] + [stats[k] * mine_share + theirs[k] * their_share for k in (1, 2)])
    every = exchange(jnp.broadcast_to(joined[None], (NZ, *joined.shape)), Z_GROUPS)

    dkv, own_part, other_part = backward(at, kv, own, other, expo, prob_grads, stats, every)
    received = swap_cores(other_part)
    dkv = [dkv[0]] + [shift_x(dkv[n], -n) for n in range(1, NX)]

    def terms(steps, halves, dtype):
        return context_terms(at, *weights, dkv, steps, halves, dtype)

    def halve(part, bit):
        half = part.shape[0] // 2
        return part[:half] + flip_z(part[half:].astype(BF16), bit).astype(F32)

    far_upper, far_lower = terms((2,), 2, BF16)
    add_upper, add_lower = shift_y(far_upper, 1), shift_y(far_lower, -1)
    part = own_part + received.astype(F32)
    part = halve(part, 1)
    part = halve(after(part, far_upper), 2)

    up, down, kept = terms((1, 3, 0), 1, F32)
    part = halve(after(part, kept), 4)
    up, down = join_terms(up, down, add_upper, add_lower)
    from_below, from_above = shift_y(up, 1), shift_y(down, -1)
    part = after(part, up)
    part = part.astype(BF16).reshape(NX, lat, 2 * DH)
    pieces = [part[0]] + [shift_x(part[n], -n) for n in range(1, NX)]
    attended, query_grad = place_heads(at, pieces)
    kept = after(kept, attended)

    return (attended, finish(kept, from_below, from_above), query_grad)


def solution(mesh):
    return jax.shard_map(
        shards,
        mesh=mesh,
        in_specs=(
            P("ctx", "tp"),
            P(None, "tp"),
            P(None, "tp"),
            P("ctx", "tp"),
            P(),
            P("ctx", "tp"),
        ),
        out_specs=(P("ctx", "tp"), P("ctx", "tp"), P("ctx", "tp")),
        check_vma=False,
    )
```
